32 devices in a mesh: gx: 4 (over x, core), gy: 2 (over y), obs: 4 (over z).
Axes of the slice: x: 2, y: 2, z: 4, core: 2. Of those that a mesh axis runs over, the one named last changes fastest.
Arguments:
- control: float32 [4, 4, 256, 512], P(None, 'obs', 'gy', 'gx'), may hold values from -6 to 6
- diffusivity: float32 [2, 4, 256, 512], P(None, 'obs', 'gy', 'gx'), may hold values from 0.12 to 0.245
- prof_tile: int32 [4096, 1], P(('gx', 'gy')), may hold values from 0 to 7; in each aligned block of 512 rows (0 to 511, 512 to 1023, ...) at most 128 rows name the same one
- prof_cell: int32 [4096], P(('gx', 'gy')), may hold values from 0 to 16383
- obs_prof: int32 [16384], P(('gx', 'gy', 'obs')), may hold values from 0 to 511
- obs_field: int32 [16384], P(('gx', 'gy', 'obs')), may hold values from 0 to 3
- obs_level: int32 [16384], P(('gx', 'gy', 'obs')), may hold values from 0 to 2
- obs_weight: float32 [16384], P(('gx', 'gy', 'obs')), may hold values from 0 to 1
- innovation: float32 [16384], P(('gx', 'gy', 'obs')), may hold values from -6 to 6
- obs_precision: float32 [16384], P(('gx', 'gy', 'obs')), may hold values from 0.25 to 4
Outputs:
- gradient: float32 [4, 4, 256, 512], P(None, 'obs', 'gy', 'gx')
- departures: float32 [16384], P(('gx', 'gy', 'obs'))
The draws below stay inside these ranges and needn't reach their ends.
Inputs may be any that keep to these rules, and one draw needn't show every extreme that they name: `prof_tile`: in each aligned block of 512 rows (the profiles of one tile) no tile is named by more than 128 rows; in some blocks one tile is named by exactly 128 rows.
All inputs are finite; a program needn't handle non-finite values.
Results may differ from the reference program's by a relative error of at most 0.00002.
Values sent between devices are 32-bit elements; how exact they have to be, the bound alone decides.
A program may use at most 64 MiB of HBM per device.

```python
import math
import jax
import jax.numpy as jnp
import numpy as np
from jax import lax

F = 4
CY = 128
CX = 128
PROF_DEV = 512
OBS_DEV = 512
STEPS = 10
LEV = 4
NY = 256
NX = 512
PROFILES = 4096
OBSERVATIONS = 16384
CAP = 128
N_GX = 4
N_GY = 2
N_OBS = 4


def place_ends(result, stream_key, smallest, top_value):
    longest = result.shape.index(max(result.shape))
    spots = []
    for shift in (0, 1):
        where = [jax.random.randint(jax.random.fold_in(stream_key, axis), (), 0, length) for axis, length in enumerate(result.shape)]
        where[longest] = (where[longest] + shift) % result.shape[longest]
        spots.append(tuple(where))
    return result.at[spots[0]].set(smallest).at[spots[1]].set(top_value)


def block_levels(key, shape, pieces, smallest, largest):
    loudness, own = 1.0, jax.random.fold_in(key, 6)
    for dim, blocks in pieces:
        draws = jnp.exp(jax.random.uniform(jax.random.fold_in(own, dim), (blocks,), jnp.float32, smallest / len(pieces), largest / len(pieces)))
        loudness = loudness * jnp.repeat(draws, shape[dim] // blocks).reshape([-1 if axis == dim else 1 for axis in range(len(shape))])
    return loudness


def routed_block(stream_key, own, number, rows, count, top, bound, slope):
    sequence = jax.random.permutation(stream_key, count)
    crowded, usual = portions_of(count, rows * top, bound, slope, True), portions_of(count, rows * top, bound, slope, False)
    places = jnp.arange(count)

    def named(lengths, offset_by):
        used = int((lengths > 0).sum())
        fixed = max(1, used // 4)
        moved = fixed + (places - fixed + offset_by * (used - fixed)) % max(1, count - fixed)
        return jnp.zeros((count,), jnp.int32).at[sequence[jnp.where(places < fixed, places, moved)]].set(jnp.asarray(lengths, jnp.int32))

    lengths = jnp.where(number % 4 == 0, named(crowded, number // 4), named(usual, number - number // 4 - 1))
    mixed = jax.random.permutation(jax.random.fold_in(own, 3), count)
    donor, receiver = mixed[0:count // 2 * 2:2], mixed[1:count // 2 * 2:2]
    slack = jnp.minimum(lengths[donor] - 1, bound - lengths[receiver]) // 2
    slack = jnp.where((donor == sequence[0]) | (receiver == sequence[0]) | (lengths[receiver] == 0), 0, jnp.maximum(slack, 0))
    moved = jax.random.randint(jax.random.fold_in(own, 4), (count // 2,), 0, 1 << 20) % (slack + 1)
    lengths = lengths.at[donor].add(-moved).at[receiver].add(moved)
    items = jnp.searchsorted(jnp.cumsum(lengths), jnp.arange(rows * top), side="right").astype(jnp.int32)
    listing = items.reshape(top, rows).T
    listing = listing[jax.random.permutation(jax.random.fold_in(own, 1), rows)]
    offset_by = jax.random.randint(jax.random.fold_in(own, 2), (rows, 1), 0, top)
    return jnp.take_along_axis(listing, (jnp.arange(top)[None, :] + offset_by) % top, axis=1)


def portions_of(amount, total, reach, skew, full):
    loads = [(1 << 20) // math.isqrt(grade ** skew) + 1 for grade in range(1, amount + 1)]
    largest = reach if full else min(reach, max(-(-total // amount), total * loads[0] // sum(loads)))
    least = 1 if total - largest >= amount - 1 else 0
    counts, spare = [largest] + [least] * (amount - 1), total - largest - least * (amount - 1)
    while spare > 0:
        candidates = [i for i in range(1, amount) if counts[i] < largest] or [i for i in range(1, amount) if counts[i] < reach]
        mass, budget = sum([loads[i] for i in candidates]), spare
        for i in candidates:
            more = min(reach - counts[i], max(1, budget * loads[i] // mass), spare)
            counts[i] = counts[i] + more
            spare = spare - more
    return np.array(counts)


def noise(rng, shape, deviation, reach, cuts=(), held_as=jnp.bfloat16):
    factor_of = block_levels(rng, shape, cuts, -0.22, 0.18) if cuts else 1.0
    values = jax.random.normal(rng, shape, jnp.float32) * deviation * factor_of
    return jnp.minimum(jnp.maximum(values, -reach), reach).astype(held_as)


def setup_inputs(seed: int = 0) -> dict:
    keys = jax.random.split(jax.random.key(seed), 11)
    control = noise(keys[0], (F, LEV, NY, NX), 1.0, 6.0, ((1, 4), (2, 2), (3, 4)), jnp.float32)
    diffusivity = jnp.clip(jnp.exp(math.log(0.245) - 0.7137665 * jax.random.uniform(keys[1], (2, LEV, NY, NX), jnp.float32) ** block_levels(keys[1], (2, LEV, NY, NX), ((1, 4), (2, 2), (3, 4)), -0.2, 0.2)), 0.12, 0.245)
    prof_tile_keys = jax.random.split(jax.random.fold_in(keys[2], 1), PROFILES // PROF_DEV)
    prof_tile_turns = jax.random.permutation(jax.random.fold_in(keys[2], 3), PROFILES // PROF_DEV)
    prof_tile = jax.vmap(lambda own, number: routed_block(jax.random.fold_in(keys[2], 2), own, number, PROF_DEV, N_GX * N_GY, 1, CAP, 2))(prof_tile_keys, prof_tile_turns).reshape((PROFILES, 1))
    prof_cell = place_ends(jax.random.randint(keys[3], (PROFILES,), 0, CY * CX), jax.random.fold_in(keys[3], 1), 0, (CY * CX) - 1).astype(jnp.int32)
    obs_prof = place_ends(jax.random.randint(keys[4], (OBSERVATIONS,), 0, PROF_DEV), jax.random.fold_in(keys[4], 1), 0, PROF_DEV - 1).astype(jnp.int32)
    obs_field = place_ends(jax.random.randint(keys[5], (OBSERVATIONS,), 0, F), jax.random.fold_in(keys[5], 1), 0, F - 1).astype(jnp.int32)
    obs_level = place_ends(jax.random.randint(keys[6], (OBSERVATIONS,), 0, LEV - 1), jax.random.fold_in(keys[6], 1), 0, (LEV - 1) - 1).astype(jnp.int32)
    obs_weight = jnp.clip(1.0 * jax.random.uniform(keys[7], (OBSERVATIONS,), jnp.float32) ** block_levels(keys[7], (OBSERVATIONS,), ((0, 32),), -0.2, 0.2), 0.0, 1.0)
    innovation = noise(keys[8], (OBSERVATIONS,), 1.0, 6.0, ((0, 32),), jnp.float32)
    obs_precision = jnp.clip(jnp.exp(math.log(4.0) - 2.7725887 * jax.random.uniform(keys[9], (OBSERVATIONS,), jnp.float32) ** block_levels(keys[9], (OBSERVATIONS,), ((0, 32),), -0.2, 0.2)), 0.25, 4.0)
    return dict(control=control, diffusivity=diffusivity, prof_tile=prof_tile, prof_cell=prof_cell, obs_prof=obs_prof, obs_field=obs_field, obs_level=obs_level, obs_weight=obs_weight, innovation=innovation, obs_precision=obs_precision)


def advance(values, east_rate, north_rate):
    east_flux = east_rate * (jnp.roll(values, -1, 2) - values)
    west_flux = jnp.roll(east_rate, 1, 2) * (jnp.roll(values, 1, 2) - values)
    north_flux = north_rate * (jnp.roll(values, -1, 1) - values)
    south_flux = jnp.roll(north_rate, 1, 1) * (jnp.roll(values, 1, 1) - values)
    return values + east_flux + west_flux + north_flux + south_flux


def diffuse(field, east_rate, north_rate):
    def smooth(field_plane):
        def sweep(step_index, values):
            return advance(values, east_rate, north_rate)
        return lax.fori_loop(0, STEPS, sweep, field_plane)
    return lax.map(smooth, field)


def reference(control, diffusivity, prof_tile, prof_cell, obs_prof, obs_field, obs_level, obs_weight, innovation, obs_precision):
    row_index = jnp.arange(NY)
    east_rate = diffusivity[0]
    north_rate = diffusivity[1] * (row_index != NY - 1).astype(jnp.float32)[None, :, None]
    increment = diffuse(control, east_rate, north_rate)
    holder_of = prof_tile[:, 0]
    lat_index = (holder_of % N_GY) * CY + prof_cell // CX
    lon_index = (holder_of // N_GY) * CX + prof_cell % CX
    columns = increment[:, :, lat_index, lon_index]
    owner_tile = jnp.arange(OBSERVATIONS, dtype=jnp.int32) // (OBS_DEV * N_OBS)
    profile = owner_tile * PROF_DEV + obs_prof
    flat_columns = columns.reshape(-1)
    lower_index = (obs_field * LEV + obs_level) * PROFILES + profile
    upper_index = lower_index + PROFILES
    observed = obs_weight * flat_columns[lower_index] + (1.0 - obs_weight) * flat_columns[upper_index]
    departures = obs_precision * (observed - innovation)
    adjoint = jnp.zeros((F * LEV * PROFILES,), jnp.float32)
    adjoint = adjoint.at[lower_index].add(obs_weight * departures)
    adjoint = adjoint.at[upper_index].add((1.0 - obs_weight) * departures)
    adjoint = adjoint.reshape(F, LEV, PROFILES)
    pulled = jnp.zeros(control.shape, jnp.float32).at[:, :, lat_index, lon_index].add(adjoint)
    gradient = control + diffuse(pulled, east_rate, north_rate)
    return gradient, departures
```

```python
import functools

import jax
import jax.numpy as jnp
from jax import lax
from jax.experimental import pallas as pl
from jax.experimental.pallas import tpu as pltpu
from jax.sharding import PartitionSpec as P

STEPS = 10
HALO = 16
LANES = 128
GROUP = 8
CHUNK = 8
MESH = pl.DeviceIdType.MESH


def halves(value, size):
    if size & (size - 1) == 0:
        return value >> (size.bit_length() - 1), value & (size - 1)
    return value // size, value % size


def two_parts(value):
    high = value.astype(jnp.bfloat16).astype(jnp.float32)
    return high, value - high


def kernel(
    nx, ny, nz,
    ctrl, diff, ptile, pcell, oprof, ofield, olevel, oweight, innov, oprec,
    grad_out, dep_out,
    pack_e, pack_w, w_ext, e_ext, south_c, north_c, south_d, north_d,
    codes, field_a, field_b, rate_e, rate_w, rate_n, rate_0,
    gather_lhs, gathered, col_in, col_all, adj_part, adj_in, adj_all, spread,
    halo_send, halo_recv, code_send, code_recv, col_send, col_recv,
    lev_send, lev_recv, red_send, red_recv, adj_send, adj_recv,
):
    fields, _, cy, cx = ctrl.shape
    tiles = nx * ny
    rows = cy + 2 * HALO
    gx, gy, gz = lax.axis_index("gx"), lax.axis_index("gy"), lax.axis_index("obs")
    me = gx * ny + gy
    east, west = lax.rem(gx + 1, nx), lax.rem(gx + nx - 1, nx)
    north, south = lax.rem(gy + 1, ny), lax.rem(gy + ny - 1, ny)

    def tile_device(tile):
        return {"gx": lax.div(tile, ny), "gy": lax.rem(tile, ny), "obs": gz}

    def level_device(level):
        return {"gx": gx, "gy": gy, "obs": level}

    def other_tile(i):
        return lax.rem(me + i, tiles)

    def other_level(i):
        return lax.rem(gz + i, nz)

    barrier = pltpu.get_barrier_semaphore()

    @pl.loop(1, tiles)
    def _(i):
        pl.semaphore_signal(barrier, inc=1, device_id=tile_device(other_tile(i)), device_id_type=MESH)

    @pl.loop(1, nz)
    def _(i):
        pl.semaphore_signal(barrier, inc=1, device_id=level_device(other_level(i)), device_id_type=MESH)

    lane = lax.broadcasted_iota(jnp.int32, (cy, LANES), 1)
    first = jnp.zeros((cy, LANES), jnp.float32)
    last = jnp.zeros((cy, LANES), jnp.float32)
    for j in range(fields + 2):
        plane = ctrl[j, 0] if j < fields else diff[j - fields, 0]
        here = (lane >= HALO * j) & (lane < HALO * (j + 1))
        last = jnp.where(here, pltpu.roll(plane, (HALO * (j + 1)) % LANES, 1), last)
        moved = plane if j == 0 else pltpu.roll(plane, HALO * j, 1)
        first = jnp.where(here, moved, first)
    pack_e[...] = last
    pack_w[...] = first
    codes[me, 0:1] = ptile[...]
    codes[me, 1:2] = pcell[...]

    pl.semaphore_wait(barrier, tiles - 1 + nz - 1)

    low, high = pl.ds(0, HALO), pl.ds(cy - HALO, HALO)
    ext_low, ext_mid, ext_high = pl.ds(0, HALO), pl.ds(HALO, cy), pl.ds(HALO + cy, HALO)
    routes = (
        (pack_e, w_ext.at[ext_mid], east, gy),
        (pack_w, e_ext.at[ext_mid], west, gy),
        (ctrl.at[:, 0, high], south_c, gx, north),
        (ctrl.at[:, 0, low], north_c, gx, south),
        (diff.at[:, 0, high], south_d, gx, north),
        (diff.at[:, 0, low], north_d, gx, south),
        (pack_e.at[high], w_ext.at[ext_low], east, north),
        (pack_e.at[low], w_ext.at[ext_high], east, south),
        (pack_w.at[high], e_ext.at[ext_low], west, north),
        (pack_w.at[low], e_ext.at[ext_high], west, south),
    )
    halo_copies = [
        pltpu.make_async_remote_copy(
            src_ref=src,
            dst_ref=dst,
            send_sem=halo_send.at[n],
            recv_sem=halo_recv.at[n],
            device_id={"gx": to_x, "gy": to_y, "obs": gz},
            device_id_type=MESH,
        )
        for n, (src, dst, to_x, to_y) in enumerate(routes)
    ]
    for copy in halo_copies:
        copy.start()

    def tile_copy(src, dst, send, recv, i, source):
        return pltpu.make_async_remote_copy(
            src_ref=src,
            dst_ref=dst.at[source],
            send_sem=send.at[i],
            recv_sem=recv.at[source],
            device_id=tile_device(other_tile(i)),
            device_id_type=MESH,
        )

    def level_copy(src, dst, send, recv, i, source):
        return pltpu.make_async_remote_copy(
            src_ref=src,
            dst_ref=dst.at[source],
            send_sem=send.at[i],
            recv_sem=recv.at[source],
            device_id=level_device(other_level(i)),
            device_id_type=MESH,
        )

    @pl.loop(1, tiles)
    def _(i):
        tile_copy(codes.at[me], codes, code_send, code_recv, i, me).start()

    for copy in halo_copies:
        copy.wait()

    lane_x = lax.broadcasted_iota(jnp.int32, (rows, LANES), 1)

    def aux_plane(j):
        from_east = e_ext[...] if j == 0 else pltpu.roll(e_ext[...], LANES - HALO * j, 1)
        from_west = pltpu.roll(w_ext[...], LANES - HALO * (j + 1), 1)
        rest = jnp.where(lane_x >= LANES - HALO, from_west, 0.0)
        return jnp.where(lane_x < HALO, from_east, rest)

    def put_plane(target, s, plane):
        target[pl.ds(s, rows, stride=GROUP), :] = plane

    for f in range(fields):
        field_a[pl.ds(f, HALO, stride=GROUP), :] = south_c[f]
        field_a[pl.ds(GROUP * HALO + f, cy, stride=GROUP), :] = ctrl[f, 0]
        field_a[pl.ds(GROUP * (HALO + cy) + f, HALO, stride=GROUP), :] = north_c[f]
        put_plane(field_a, fields + f, aux_plane(f))

    lat_count = ny * cy
    row_x = lax.broadcasted_iota(jnp.int32, (rows, LANES), 0) + (gy * cy - HALO)
    wall = (row_x == lat_count - 1) | (row_x == -1)

    def main_plane(k):
        return jnp.concatenate([south_d[k], diff[k, 0], north_d[k]], axis=0)

    e_main, e_aux = main_plane(0), aux_plane(fields)
    n_main = jnp.where(wall, 0.0, main_plane(1))
    n_aux = jnp.where(wall, 0.0, aux_plane(fields + 1))
    w_main = pltpu.roll(jnp.where(lane_x == LANES - 1, e_aux, e_main), 1, 1)
    w_aux = pltpu.roll(jnp.where(lane_x == LANES - 1, e_main, e_aux), 1, 1)
    c_main = 1.0 - (e_main + w_main + n_main + pltpu.roll(n_main, 1, 0))
    c_aux = 1.0 - (e_aux + w_aux + n_aux + pltpu.roll(n_aux, 1, 0))
    for target, main, aux in (
        (rate_e, e_main, e_aux),
        (rate_w, w_main, w_aux),
        (rate_n, n_main, n_aux),
        (rate_0, c_main, c_aux),
    ):
        for f in range(fields):
            put_plane(target, f, main)
            put_plane(target, fields + f, aux)

    size = CHUNK * GROUP
    lane_c = lax.broadcasted_iota(jnp.int32, (size, LANES), 1)
    margin = HALO - STEPS - 2
    chunks = (rows - 2 * margin) // CHUNK

    def step(old, new):
        @pl.loop(0, chunks)
        def _(c):
            at = pl.multiple_of((margin + c * CHUNK) * GROUP, GROUP)
            here, before = pl.ds(at, size), pl.ds(at - GROUP, size)
            after = pl.ds(at + GROUP, size)
            v = old[here, :]
            swapped = pltpu.roll(v.reshape(CHUNK, GROUP, LANES), fields, 1).reshape(size, LANES)
            v_west = pltpu.roll(jnp.where(lane_c == LANES - 1, swapped, v), 1, 1)
            v_east = pltpu.roll(jnp.where(lane_c == 0, swapped, v), LANES - 1, 1)
            new[here, :] = (
                rate_0[here, :] * v
                + rate_e[here, :] * v_east
                + rate_w[here, :] * v_west
                + rate_n[here, :] * old[after, :]
                + rate_n[before, :] * old[before, :]
            )

    def diffuse():
        @pl.loop(0, STEPS // 2)
        def _(_):
            step(field_a, field_b)
            step(field_b, field_a)

    diffuse()

    for f in range(fields):
        turned = field_a[pl.ds(GROUP * HALO + f, cy, stride=GROUP), :].T
        big, small = two_parts(turned)
        gather_lhs[pl.ds(f * cx, cx), 0:cy] = big.astype(jnp.bfloat16)
        gather_lhs[pl.ds(f * cx, cx), cy : 2 * cy] = small.astype(jnp.bfloat16)

    profs = codes.shape[2]
    row_p = lax.broadcasted_iota(jnp.int32, (cy, profs), 0)

    def gather_for(tile):
        holder, cell = codes[tile, 0:1], codes[tile, 1:2]
        y, x = halves(cell, cx)
        y = jnp.where(holder == me, y, -1)
        pick = (row_p == y).astype(jnp.float32).astype(jnp.bfloat16)
        found = jnp.dot(
            gather_lhs[...],
            jnp.concatenate([pick, pick], axis=0),
            preferred_element_type=jnp.float32,
        )
        column = row_p == x
        sums = [
            jnp.sum(jnp.where(column, found[f * cx : (f + 1) * cx], 0.0), axis=0, keepdims=True)
            for f in range(fields)
        ]
        return jnp.concatenate(sums + [jnp.zeros((GROUP - fields, profs), jnp.float32)], axis=0)

    @pl.loop(1, tiles)
    def _(i):
        tile = other_tile(i)
        copy = tile_copy(codes.at[tile], codes, code_send, code_recv, i, tile)
        copy.wait_recv()
        gathered[i] = gather_for(tile)
        tile_copy(gathered.at[i], col_in, col_send, col_recv, i, me).start()

    col_in[me] = gather_for(me)

    total = col_in[me]
    gathered[0] = total

    @pl.loop(1, tiles)
    def _(i):
        tile = other_tile(i)
        tile_copy(gathered.at[i], col_in, col_send, col_recv, i, tile).wait_recv()
        gathered[0] = gathered[0] + col_in[tile]

    col_all[gz] = gathered[0]

    @pl.loop(1, nz)
    def _(i):
        level_copy(col_all.at[gz], col_all, lev_send, lev_recv, i, gz).start()

    obs_count = oprof.shape[1]
    match = lax.broadcasted_iota(jnp.int32, (profs, obs_count), 0) == oprof[...]
    match = match.astype(jnp.float32).astype(jnp.bfloat16)
    slot = lax.broadcasted_iota(jnp.int32, (nz * GROUP, obs_count), 0)
    wanted = olevel[...] * GROUP + ofield[...]
    weight = oweight[...]
    mix = jnp.where(slot == wanted, weight, jnp.where(slot == wanted + GROUP, 1.0 - weight, 0.0))

    @pl.loop(1, nz)
    def _(i):
        level = other_level(i)
        level_copy(col_all.at[level], col_all, lev_send, lev_recv, i, level).wait_recv()

    wide = nz * GROUP
    big, small = two_parts(col_all[...].reshape(wide, profs))
    both = jnp.concatenate([big, small], axis=0).astype(jnp.bfloat16)
    seen = jnp.dot(both, match, preferred_element_type=jnp.float32)
    seen = seen[0:wide] + seen[wide:]
    observed = jnp.sum(mix * seen, axis=0, keepdims=True)
    departures = oprec[...] * (observed - innov[...])
    dep_out[...] = departures
    big, small = two_parts(mix * departures)
    both = jnp.concatenate([big, small], axis=0).astype(jnp.bfloat16)
    back = lax.dot_general(
        both, match, (((1,), (1,)), ((), ())), preferred_element_type=jnp.float32
    )
    adj_part[...] = (back[0:wide] + back[wide:]).reshape(nz, GROUP, profs)

    @pl.loop(1, nz)
    def _(i):
        level_copy(adj_part.at[other_level(i)], adj_in, red_send, red_recv, i, gz).start()

    gathered[0] = adj_part[gz]

    @pl.loop(1, nz)
    def _(i):
        level = other_level(i)
        level_copy(adj_part.at[level], adj_in, red_send, red_recv, i, level).wait_recv()
        gathered[0] = gathered[0] + adj_in[level]

    adj_all[me] = gathered[0]

    @pl.loop(1, tiles)
    def _(i):
        tile_copy(adj_all.at[me], adj_all, adj_send, adj_recv, i, me).start()

    row_r = lax.broadcasted_iota(jnp.int32, (rows, profs), 0)
    row_c = lax.broadcasted_iota(jnp.int32, (2 * LANES, profs), 0)

    def scatter_from(tile):
        holder, cell = codes[tile, 0:1], codes[tile, 1:2]
        holder_x, holder_y = halves(holder, ny)
        y, x = halves(cell, cx)
        near = row_r == (holder_y - gy) * cy + y + HALO
        side = ((holder_x == east) & (x < cx // 2)) | ((holder_x == west) & (x >= cx // 2))
        place = jnp.where(holder_x == gx, x, jnp.where(side, LANES + x, -1))
        spots = (row_c == place).astype(jnp.float32).astype(jnp.bfloat16)
        amounts = adj_all[tile]
        big, small = two_parts(amounts)
        lines = []
        for f in range(fields):
            parts = [
                jnp.where(near, part[f : f + 1], 0.0).astype(jnp.bfloat16) for part in (big, small)
            ]
            lines.append(jnp.concatenate(parts, axis=1))
        return lax.dot_general(
            jnp.concatenate(lines, axis=0),
            jnp.concatenate([spots, spots], axis=1),
            (((1,), (1,)), ((), ())),
            preferred_element_type=jnp.float32,
        )

    spread[...] = scatter_from(me)

    @pl.loop(1, tiles)
    def _(i):
        tile = other_tile(i)
        tile_copy(adj_all.at[me], adj_all, adj_send, adj_recv, i, tile).wait_recv()
        spread[...] += scatter_from(tile)

    for f in range(fields):
        put_plane(field_a, f, spread[pl.ds(f * rows, rows), 0:LANES])
        put_plane(field_a, fields + f, spread[pl.ds(f * rows, rows), LANES : 2 * LANES])

    diffuse()

    for f in range(fields):
        grad_out[f, 0] = field_a[pl.ds(GROUP * HALO + f, cy, stride=GROUP), :]

    @pl.loop(1, tiles)
    def _(i):
        tile_copy(codes.at[me], codes, code_send, code_recv, i, me).wait_send()
        tile_copy(gathered.at[i], col_in, col_send, col_recv, i, me).wait_send()
        tile_copy(adj_all.at[me], adj_all, adj_send, adj_recv, i, me).wait_send()

    @pl.loop(1, nz)
    def _(i):
        level_copy(col_all.at[gz], col_all, lev_send, lev_recv, i, gz).wait_send()
        level_copy(adj_part.at[other_level(i)], adj_in, red_send, red_recv, i, gz).wait_send()


def per_device(
    nx, ny, nz,
    control,
    diffusivity,
    prof_tile,
    prof_cell,
    obs_prof,
    obs_field,
    obs_level,
    obs_weight,
    innovation,
    obs_precision,
):
    fields, _, cy, cx = control.shape
    profs = prof_cell.shape[0]
    obs_count = obs_prof.shape[0]
    tiles = nx * ny
    rows = cy + 2 * HALO
    f32 = jnp.float32

    def plane(*shape):
        return pltpu.VMEM(shape, f32)

    def flags(count):
        return pltpu.SemaphoreType.DMA((count,))

    scratch = [
        plane(cy, LANES), plane(cy, LANES), plane(rows, LANES), plane(rows, LANES),
        plane(fields, HALO, LANES), plane(fields, HALO, LANES),
        plane(2, HALO, LANES), plane(2, HALO, LANES),
        pltpu.VMEM((tiles, 2, profs), jnp.int32),
    ]
    scratch += [plane(rows * GROUP, LANES)] * 6
    scratch += [
        pltpu.VMEM((fields * cx, 2 * cy), jnp.bfloat16),
        plane(tiles, GROUP, profs),
        plane(tiles, GROUP, profs),
        plane(nz, GROUP, profs),
        plane(nz, GROUP, profs),
        plane(nz, GROUP, profs),
        plane(tiles, GROUP, profs),
        plane(fields * rows, 2 * LANES),
        flags(10), flags(10),
        flags(tiles), flags(tiles), flags(tiles), flags(tiles),
        flags(nz), flags(nz), flags(nz), flags(nz),
        flags(tiles), flags(tiles),
    ]
    spread, departures = pl.pallas_call(
        functools.partial(kernel, nx, ny, nz),
        out_shape=(
            jax.ShapeDtypeStruct(control.shape, f32),
            jax.ShapeDtypeStruct((1, obs_count), f32),
        ),
        in_specs=[pl.BlockSpec(memory_space=pltpu.VMEM)] * 10,
        out_specs=(pl.BlockSpec(memory_space=pltpu.VMEM),) * 2,
        scratch_shapes=scratch,
        compiler_params=pltpu.CompilerParams(
            collective_id=0, has_side_effects=True, vmem_limit_bytes=48 * 1024 * 1024
        ),
    )(
        control,
        diffusivity,
        prof_tile.reshape(1, profs),
        prof_cell.reshape(1, profs),
        obs_prof.reshape(1, obs_count),
        obs_field.reshape(1, obs_count),
        obs_level.reshape(1, obs_count),
        obs_weight.reshape(1, obs_count),
        innovation.reshape(1, obs_count),
        obs_precision.reshape(1, obs_count),
    )
    return (control + spread, departures.reshape(obs_count))


def solution(mesh):
    nx, ny, nz = mesh.shape["gx"], mesh.shape["gy"], mesh.shape["obs"]
    in_specs = (
        P(None, "obs", "gy", "gx"),
        P(None, "obs", "gy", "gx"),
        P(("gx", "gy"), None),
        P(("gx", "gy")),
        P(("gx", "gy", "obs")),
        P(("gx", "gy", "obs")),
        P(("gx", "gy", "obs")),
        P(("gx", "gy", "obs")),
        P(("gx", "gy", "obs")),
        P(("gx", "gy", "obs")),
    )
    out_specs = (P(None, "obs", "gy", "gx"), P(("gx", "gy", "obs")))
    return jax.shard_map(
        functools.partial(per_device, nx, ny, nz),
        mesh=mesh,
        in_specs=in_specs,
        out_specs=out_specs,
        check_vma=False,
    )
```

```python
import functools

import jax
import jax.numpy as jnp
from jax import lax
from jax.experimental import pallas as pl
from jax.experimental.pallas import tpu as pltpu
from jax.sharding import PartitionSpec as P

STEPS = 10
HALO = 16
LANES = 128
GROUP = 8
CHUNK = 38
MESH = pl.DeviceIdType.MESH


def halves(value, size):
    if size & (size - 1) == 0:
        return value >> (size.bit_length() - 1), value & (size - 1)
    return value // size, value % size


def two_parts(value):
    high = value.astype(jnp.bfloat16).astype(jnp.float32)
    return high, value - high


def kernel(
    nx, ny, nz,
    ctrl_in, diff_in, ptile_in, pcell_in, oprof_in, ofield_in, olevel_in, oweight_in, innov_in, oprec_in,
    grad_out, dep_out,
    ctrl, diff, ptile, pcell, oprof, ofield, olevel, oweight, innov, oprec, fetched, match, mix,
    pack_e, pack_w, w_ext, e_ext, south_c, north_c, south_d, north_d,
    codes, field_a, field_b, rate_e, rate_w, rate_n, rate_0,
    gather_lhs, gathered, col_in, col_all, adj_part, adj_in, adj_all, spread,
    halo_send, halo_recv, code_send, code_recv, col_send, col_recv,
    lev_send, lev_recv, red_send, red_recv, adj_send, adj_recv,
):
    fields, _, cy, cx = ctrl.shape
    tiles = nx * ny
    rows = cy + 2 * HALO
    gx, gy, gz = lax.axis_index("gx"), lax.axis_index("gy"), lax.axis_index("obs")
    me = gx * ny + gy
    east, west = lax.rem(gx + 1, nx), lax.rem(gx + nx - 1, nx)
    north, south = lax.rem(gy + 1, ny), lax.rem(gy + ny - 1, ny)

    def tile_device(tile):
        return {"gx": lax.div(tile, ny), "gy": lax.rem(tile, ny), "obs": gz}

    def level_device(level):
        return {"gx": gx, "gy": gy, "obs": level}

    def other_tile(i):
        return lax.rem(me + i, tiles)

    def other_level(i):
        return lax.rem(gz + i, nz)

    fetches = [
        pltpu.make_async_copy(src, dst, fetched.at[n])
        for n, (src, dst) in enumerate((
            (ctrl_in, ctrl), (diff_in, diff), (ptile_in, ptile), (pcell_in, pcell),
            (oprof_in, oprof), (ofield_in, ofield), (olevel_in, olevel),
            (oweight_in, oweight), (innov_in, innov), (oprec_in, oprec),
        ))
    ]
    for fetch in fetches:
        fetch.start()

    barrier = pltpu.get_barrier_semaphore()

    @pl.loop(1, tiles)
    def _(i):
        pl.semaphore_signal(barrier, inc=1, device_id=tile_device(other_tile(i)), device_id_type=MESH)

    @pl.loop(1, nz)
    def _(i):
        pl.semaphore_signal(barrier, inc=1, device_id=level_device(other_level(i)), device_id_type=MESH)

    for fetch in fetches[0:4]:
        fetch.wait()

    lane = lax.broadcasted_iota(jnp.int32, (cy, LANES), 1)
    first = jnp.zeros((cy, LANES), jnp.float32)
    last = jnp.zeros((cy, LANES), jnp.float32)
    for j in range(fields + 2):
        plane = ctrl[j, 0] if j < fields else diff[j - fields, 0]
        here = (lane >= HALO * j) & (lane < HALO * (j + 1))
        last = jnp.where(here, pltpu.roll(plane, (HALO * (j + 1)) % LANES, 1), last)
        moved = plane if j == 0 else pltpu.roll(plane, HALO * j, 1)
        first = jnp.where(here, moved, first)
    pack_e[...] = last
    pack_w[...] = first
    codes[me, 0:1] = ptile[...]
    codes[me, 1:2] = pcell[...]

    pl.semaphore_wait(barrier, tiles - 1 + nz - 1)

    low, high = pl.ds(0, HALO), pl.ds(cy - HALO, HALO)
    ext_low, ext_mid, ext_high = pl.ds(0, HALO), pl.ds(HALO, cy), pl.ds(HALO + cy, HALO)
    routes = (
        (pack_e, w_ext.at[ext_mid], east, gy),
        (pack_w, e_ext.at[ext_mid], west, gy),
        (ctrl.at[:, 0, high], south_c, gx, north),
        (ctrl.at[:, 0, low], north_c, gx, south),
        (diff.at[:, 0, high], south_d, gx, north),
        (diff.at[:, 0, low], north_d, gx, south),
        (pack_e.at[high], w_ext.at[ext_low], east, north),
        (pack_e.at[low], w_ext.at[ext_high], east, south),
        (pack_w.at[high], e_ext.at[ext_low], west, north),
        (pack_w.at[low], e_ext.at[ext_high], west, south),
    )
    halo_copies = [
        pltpu.make_async_remote_copy(
            src_ref=src,
            dst_ref=dst,
            send_sem=halo_send.at[n],
            recv_sem=halo_recv.at[n],
            device_id={"gx": to_x, "gy": to_y, "obs": gz},
            device_id_type=MESH,
        )
        for n, (src, dst, to_x, to_y) in enumerate(routes)
    ]
    for copy in halo_copies:
        copy.start()

    def tile_copy(src, dst, send, recv, i, source):
        return pltpu.make_async_remote_copy(
            src_ref=src,
            dst_ref=dst.at[source],
            send_sem=send.at[i],
            recv_sem=recv.at[source],
            device_id=tile_device(other_tile(i)),
            device_id_type=MESH,
        )

    def level_copy(src, dst, send, recv, i, source):
        return pltpu.make_async_remote_copy(
            src_ref=src,
            dst_ref=dst.at[source],
            send_sem=send.at[i],
            recv_sem=recv.at[source],
            device_id=level_device(other_level(i)),
            device_id_type=MESH,
        )

    @pl.loop(1, tiles)
    def _(i):
        tile_copy(codes.at[me], codes, code_send, code_recv, i, me).start()

    for fetch in fetches[4:]:
        fetch.wait()

    profs, obs_count = codes.shape[2], oprof.shape[1]
    row_m = lax.broadcasted_iota(jnp.int32, (profs, obs_count), 0)
    match[...] = (row_m == oprof[...]).astype(jnp.float32).astype(jnp.bfloat16)
    slot = lax.broadcasted_iota(jnp.int32, (nz * GROUP, obs_count), 0)
    wanted = olevel[...] * GROUP + ofield[...]
    weight = oweight[...]
    mix[...] = jnp.where(slot == wanted, weight, jnp.where(slot == wanted + GROUP, 1.0 - weight, 0.0))

    for copy in halo_copies:
        copy.wait()

    lane_x = lax.broadcasted_iota(jnp.int32, (rows, LANES), 1)

    def aux_plane(j):
        from_east = e_ext[...] if j == 0 else pltpu.roll(e_ext[...], LANES - HALO * j, 1)
        from_west = pltpu.roll(w_ext[...], LANES - HALO * (j + 1), 1)
        rest = jnp.where(lane_x >= LANES - HALO, from_west, 0.0)
        return jnp.where(lane_x < HALO, from_east, rest)

    def put_plane(target, s, plane):
        target[pl.ds(s, rows, stride=GROUP), :] = plane

    for f in range(fields):
        field_a[pl.ds(f, HALO, stride=GROUP), :] = south_c[f]
        field_a[pl.ds(GROUP * HALO + f, cy, stride=GROUP), :] = ctrl[f, 0]
        field_a[pl.ds(GROUP * (HALO + cy) + f, HALO, stride=GROUP), :] = north_c[f]
        put_plane(field_a, fields + f, aux_plane(f))

    lat_count = ny * cy
    row_x = lax.broadcasted_iota(jnp.int32, (rows, LANES), 0) + (gy * cy - HALO)
    wall = (row_x == lat_count - 1) | (row_x == -1)

    def main_plane(k):
        return jnp.concatenate([south_d[k], diff[k, 0], north_d[k]], axis=0)

    e_main, e_aux = main_plane(0), aux_plane(fields)
    n_main = jnp.where(wall, 0.0, main_plane(1))
    n_aux = jnp.where(wall, 0.0, aux_plane(fields + 1))
    for target, main, aux in ((rate_e, e_main, e_aux), (rate_n, n_main, n_aux)):
        for f in range(fields):
            put_plane(target, f, main)
            put_plane(target, fields + f, aux)

    size = CHUNK * GROUP
    lane_c = lax.broadcasted_iota(jnp.int32, (size, LANES), 1)
    margin = HALO - STEPS - 2
    chunks = (rows - 2 * margin) // CHUNK

    def swap(v):
        return pltpu.roll(v.reshape(CHUNK, GROUP, LANES), fields, 1).reshape(size, LANES)

    def from_west(v, swapped):
        return pltpu.roll(jnp.where(lane_c == LANES - 1, swapped, v), 1, 1)

    @pl.loop(0, chunks)
    def _(c):
        at = pl.multiple_of((margin + c * CHUNK) * GROUP, GROUP)
        here, before = pl.ds(at, size), pl.ds(at - GROUP, size)
        e, n = rate_e[here, :], rate_n[here, :]
        w = from_west(e, swap(e))
        rate_w[here, :] = w
        rate_0[here, :] = 1.0 - (e + w + n + rate_n[before, :])

    def step(old, new):
        @pl.loop(0, chunks)
        def _(c):
            at = pl.multiple_of((margin + c * CHUNK) * GROUP, GROUP)
            here, before = pl.ds(at, size), pl.ds(at - GROUP, size)
            after = pl.ds(at + GROUP, size)
            v = old[here, :]
            swapped = swap(v)
            v_west = from_west(v, swapped)
            v_east = pltpu.roll(jnp.where(lane_c == 0, swapped, v), LANES - 1, 1)
            new[here, :] = (
                rate_0[here, :] * v
                + rate_e[here, :] * v_east
                + rate_w[here, :] * v_west
                + rate_n[here, :] * old[after, :]
                + rate_n[before, :] * old[before, :]
            )

    def diffuse():
        @pl.loop(0, STEPS // 2)
        def _(_):
            step(field_a, field_b)
            step(field_b, field_a)

    diffuse()

    for f in range(fields):
        turned = field_a[pl.ds(GROUP * HALO + f, cy, stride=GROUP), :].T
        big, small = two_parts(turned)
        gather_lhs[pl.ds(f * cx, cx), 0:cy] = big.astype(jnp.bfloat16)
        gather_lhs[pl.ds(f * cx, cx), cy : 2 * cy] = small.astype(jnp.bfloat16)

    row_p = lax.broadcasted_iota(jnp.int32, (cy, profs), 0)

    def gather_for(tile):
        holder, cell = codes[tile, 0:1], codes[tile, 1:2]
        y, x = halves(cell, cx)
        y = jnp.where(holder == me, y, -1)
        pick = (row_p == y).astype(jnp.float32).astype(jnp.bfloat16)
        found = jnp.dot(
            gather_lhs[...],
            jnp.concatenate([pick, pick], axis=0),
            preferred_element_type=jnp.float32,
        )
        column = row_p == x
        sums = [
            jnp.sum(jnp.where(column, found[f * cx : (f + 1) * cx], 0.0), axis=0, keepdims=True)
            for f in range(fields)
        ]
        return jnp.concatenate(sums + [jnp.zeros((GROUP - fields, profs), jnp.float32)], axis=0)

    @pl.loop(1, tiles)
    def _(i):
        tile = other_tile(i)
        copy = tile_copy(codes.at[tile], codes, code_send, code_recv, i, tile)
        copy.wait_recv()
        gathered[i] = gather_for(tile)
        tile_copy(gathered.at[i], col_in, col_send, col_recv, i, me).start()

    col_in[me] = gather_for(me)

    total = col_in[me]
    gathered[0] = total

    @pl.loop(1, tiles)
    def _(i):
        tile = other_tile(i)
        tile_copy(gathered.at[i], col_in, col_send, col_recv, i, tile).wait_recv()
        gathered[0] = gathered[0] + col_in[tile]

    col_all[gz] = gathered[0]

    @pl.loop(1, nz)
    def _(i):
        level_copy(col_all.at[gz], col_all, lev_send, lev_recv, i, gz).start()

    @pl.loop(1, nz)
    def _(i):
        level = other_level(i)
        level_copy(col_all.at[level], col_all, lev_send, lev_recv, i, level).wait_recv()

    wide = nz * GROUP
    big, small = two_parts(col_all[...].reshape(wide, profs))
    both = jnp.concatenate([big, small], axis=0).astype(jnp.bfloat16)
    seen = jnp.dot(both, match[...], preferred_element_type=jnp.float32)
    seen = seen[0:wide] + seen[wide:]
    observed = jnp.sum(mix[...] * seen, axis=0, keepdims=True)
    departures = oprec[...] * (observed - innov[...])
    dep_out[...] = departures
    big, small = two_parts(mix[...] * departures)
    both = jnp.concatenate([big, small], axis=0).astype(jnp.bfloat16)
    back = lax.dot_general(
        both, match[...], (((1,), (1,)), ((), ())), preferred_element_type=jnp.float32
    )
    adj_part[...] = (back[0:wide] + back[wide:]).reshape(nz, GROUP, profs)

    @pl.loop(1, nz)
    def _(i):
        level_copy(adj_part.at[other_level(i)], adj_in, red_send, red_recv, i, gz).start()

    gathered[0] = adj_part[gz]

    @pl.loop(1, nz)
    def _(i):
        level = other_level(i)
        level_copy(adj_part.at[level], adj_in, red_send, red_recv, i, level).wait_recv()
        gathered[0] = gathered[0] + adj_in[level]

    adj_all[me] = gathered[0]

    @pl.loop(1, tiles)
    def _(i):
        tile_copy(adj_all.at[me], adj_all, adj_send, adj_recv, i, me).start()

    row_r = lax.broadcasted_iota(jnp.int32, (rows, profs), 0)
    row_c = lax.broadcasted_iota(jnp.int32, (2 * LANES, profs), 0)

    def scatter_from(tile):
        holder, cell = codes[tile, 0:1], codes[tile, 1:2]
        holder_x, holder_y = halves(holder, ny)
        y, x = halves(cell, cx)
        near = row_r == (holder_y - gy) * cy + y + HALO
        side = ((holder_x == east) & (x < cx // 2)) | ((holder_x == west) & (x >= cx // 2))
        place = jnp.where(holder_x == gx, x, jnp.where(side, LANES + x, -1))
        spots = (row_c == place).astype(jnp.float32).astype(jnp.bfloat16)
        amounts = adj_all[tile]
        big, small = two_parts(amounts)
        lines = []
        for f in range(fields):
            parts = [
                jnp.where(near, part[f : f + 1], 0.0).astype(jnp.bfloat16) for part in (big, small)
            ]
            lines.append(jnp.concatenate(parts, axis=1))
        return lax.dot_general(
            jnp.concatenate(lines, axis=0),
            jnp.concatenate([spots, spots], axis=1),
            (((1,), (1,)), ((), ())),
            preferred_element_type=jnp.float32,
        )

    spread[...] = scatter_from(me)

    @pl.loop(1, tiles)
    def _(i):
        tile = other_tile(i)
        tile_copy(adj_all.at[me], adj_all, adj_send, adj_recv, i, tile).wait_recv()
        spread[...] += scatter_from(tile)

    for f in range(fields):
        put_plane(field_a, f, spread[pl.ds(f * rows, rows), 0:LANES])
        put_plane(field_a, fields + f, spread[pl.ds(f * rows, rows), LANES : 2 * LANES])

    diffuse()

    for f in range(fields):
        grad_out[f, 0] = field_a[pl.ds(GROUP * HALO + f, cy, stride=GROUP), :]

    @pl.loop(1, tiles)
    def _(i):
        tile_copy(codes.at[me], codes, code_send, code_recv, i, me).wait_send()
        tile_copy(gathered.at[i], col_in, col_send, col_recv, i, me).wait_send()
        tile_copy(adj_all.at[me], adj_all, adj_send, adj_recv, i, me).wait_send()

    @pl.loop(1, nz)
    def _(i):
        level_copy(col_all.at[gz], col_all, lev_send, lev_recv, i, gz).wait_send()
        level_copy(adj_part.at[other_level(i)], adj_in, red_send, red_recv, i, gz).wait_send()


def per_device(
    nx, ny, nz,
    control,
    diffusivity,
    prof_tile,
    prof_cell,
    obs_prof,
    obs_field,
    obs_level,
    obs_weight,
    innovation,
    obs_precision,
):
    fields, _, cy, cx = control.shape
    profs = prof_cell.shape[0]
    obs_count = obs_prof.shape[0]
    tiles = nx * ny
    rows = cy + 2 * HALO
    f32 = jnp.float32

    def plane(*shape):
        return pltpu.VMEM(shape, f32)

    def flags(count):
        return pltpu.SemaphoreType.DMA((count,))

    def numbers(count):
        return pltpu.VMEM((1, count), jnp.int32)

    scratch = [
        plane(*control.shape), plane(*diffusivity.shape), numbers(profs), numbers(profs),
        numbers(obs_count), numbers(obs_count), numbers(obs_count),
        plane(1, obs_count), plane(1, obs_count), plane(1, obs_count), flags(10),
        pltpu.VMEM((profs, obs_count), jnp.bfloat16), plane(nz * GROUP, obs_count),
    ]
    scratch += [
        plane(cy, LANES), plane(cy, LANES), plane(rows, LANES), plane(rows, LANES),
        plane(fields, HALO, LANES), plane(fields, HALO, LANES),
        plane(2, HALO, LANES), plane(2, HALO, LANES),
        pltpu.VMEM((tiles, 2, profs), jnp.int32),
    ]
    scratch += [plane(rows * GROUP, LANES)] * 6
    scratch += [
        pltpu.VMEM((fields * cx, 2 * cy), jnp.bfloat16),
        plane(tiles, GROUP, profs),
        plane(tiles, GROUP, profs),
        plane(nz, GROUP, profs),
        plane(nz, GROUP, profs),
        plane(nz, GROUP, profs),
        plane(tiles, GROUP, profs),
        plane(fields * rows, 2 * LANES),
        flags(10), flags(10),
        flags(tiles), flags(tiles), flags(tiles), flags(tiles),
        flags(nz), flags(nz), flags(nz), flags(nz),
        flags(tiles), flags(tiles),
    ]
    spread, departures = pl.pallas_call(
        functools.partial(kernel, nx, ny, nz),
        out_shape=(
            jax.ShapeDtypeStruct(control.shape, f32),
            jax.ShapeDtypeStruct((1, obs_count), f32),
        ),
        in_specs=[pl.BlockSpec(memory_space=pltpu.HBM)] * 10,
        out_specs=(pl.BlockSpec(memory_space=pltpu.VMEM),) * 2,
        scratch_shapes=scratch,
        compiler_params=pltpu.CompilerParams(
            collective_id=0, has_side_effects=True, vmem_limit_bytes=64 * 1024 * 1024
        ),
    )(
        control,
        diffusivity,
        prof_tile.reshape(1, profs),
        prof_cell.reshape(1, profs),
        obs_prof.reshape(1, obs_count),
        obs_field.reshape(1, obs_count),
        obs_level.reshape(1, obs_count),
        obs_weight.reshape(1, obs_count),
        innovation.reshape(1, obs_count),
        obs_precision.reshape(1, obs_count),
    )
    return (control + spread, departures.reshape(obs_count))


def solution(mesh):
    nx, ny, nz = mesh.shape["gx"], mesh.shape["gy"], mesh.shape["obs"]
    in_specs = (
        P(None, "obs", "gy", "gx"),
        P(None, "obs", "gy", "gx"),
        P(("gx", "gy"), None),
        P(("gx", "gy")),
        P(("gx", "gy", "obs")),
        P(("gx", "gy", "obs")),
        P(("gx", "gy", "obs")),
        P(("gx", "gy", "obs")),
        P(("gx", "gy", "obs")),
        P(("gx", "gy", "obs")),
    )
    out_specs = (P(None, "obs", "gy", "gx"), P(("gx", "gy", "obs")))
    return jax.shard_map(
        functools.partial(per_device, nx, ny, nz),
        mesh=mesh,
        in_specs=in_specs,
        out_specs=out_specs,
        check_vma=False,
    )
```

```python
import functools

import jax
import jax.numpy as jnp
from jax import lax
from jax.experimental import pallas as pl
from jax.experimental.pallas import tpu as pltpu
from jax.sharding import PartitionSpec as P

STEPS = 10
HALO = 16
LANES = 128
GROUP = 8
MESH = pl.DeviceIdType.MESH


def halves(value, size):
    if size & (size - 1) == 0:
        return value >> (size.bit_length() - 1), value & (size - 1)
    return value // size, value % size


def two_parts(value):
    high = value.astype(jnp.bfloat16).astype(jnp.float32)
    return high, value - high


def kernel(
    nx, ny, nz,
    ctrl_in, diff_in, ptile_in, pcell_in, oprof_in, ofield_in, olevel_in, oweight_in, innov_in, oprec_in,
    grad_out, dep_out,
    ctrl, diff, ptile, pcell, oprof, ofield, olevel, oweight, innov, oprec, fetched, match, mix,
    pack_e, pack_w, w_ext, e_ext, south_c, north_c, south_d, north_d,
    codes, field_a, field_b, rate_e, rate_w, rate_n, rate_0,
    gather_lhs, gathered, col_in, col_all, adj_part, adj_in, adj_all, spread, spots, nears,
    halo_send, halo_recv, code_send, code_recv, col_send, col_recv,
    lev_send, lev_recv, red_send, red_recv, adj_send, adj_recv,
):
    fields, _, cy, cx = ctrl.shape
    tiles = nx * ny
    rows = cy + 2 * HALO
    gx, gy, gz = lax.axis_index("gx"), lax.axis_index("gy"), lax.axis_index("obs")
    me = gx * ny + gy
    east, west = lax.rem(gx + 1, nx), lax.rem(gx + nx - 1, nx)
    north, south = lax.rem(gy + 1, ny), lax.rem(gy + ny - 1, ny)

    def tile_device(tile):
        return {"gx": lax.div(tile, ny), "gy": lax.rem(tile, ny), "obs": gz}

    def level_device(level):
        return {"gx": gx, "gy": gy, "obs": level}

    def other_tile(i):
        return lax.rem(me + i, tiles)

    def other_level(i):
        return lax.rem(gz + i, nz)

    fetches = [
        pltpu.make_async_copy(src, dst, fetched.at[n])
        for n, (src, dst) in enumerate((
            (ctrl_in, ctrl), (diff_in, diff), (ptile_in, ptile), (pcell_in, pcell),
            (oprof_in, oprof), (ofield_in, ofield), (olevel_in, olevel),
            (oweight_in, oweight), (innov_in, innov), (oprec_in, oprec),
        ))
    ]
    for fetch in fetches:
        fetch.start()

    barrier = pltpu.get_barrier_semaphore()

    @pl.loop(1, tiles)
    def _(i):
        pl.semaphore_signal(barrier, inc=1, device_id=tile_device(other_tile(i)), device_id_type=MESH)

    @pl.loop(1, nz)
    def _(i):
        pl.semaphore_signal(barrier, inc=1, device_id=level_device(other_level(i)), device_id_type=MESH)

    for fetch in fetches[0:4]:
        fetch.wait()

    lane = lax.broadcasted_iota(jnp.int32, (cy, LANES), 1)
    first = jnp.zeros((cy, LANES), jnp.float32)
    last = jnp.zeros((cy, LANES), jnp.float32)
    for j in range(fields + 2):
        plane = ctrl[j, 0] if j < fields else diff[j - fields, 0]
        here = (lane >= HALO * j) & (lane < HALO * (j + 1))
        last = jnp.where(here, pltpu.roll(plane, (HALO * (j + 1)) % LANES, 1), last)
        moved = plane if j == 0 else pltpu.roll(plane, HALO * j, 1)
        first = jnp.where(here, moved, first)
    pack_e[...] = last
    pack_w[...] = first
    codes[me, 0:1] = ptile[...]
    codes[me, 1:2] = pcell[...]

    pl.semaphore_wait(barrier, tiles - 1 + nz - 1)

    low, high = pl.ds(0, HALO), pl.ds(cy - HALO, HALO)
    ext_low, ext_mid, ext_high = pl.ds(0, HALO), pl.ds(HALO, cy), pl.ds(HALO + cy, HALO)
    routes = (
        (pack_e, w_ext.at[ext_mid], east, gy),
        (pack_w, e_ext.at[ext_mid], west, gy),
        (ctrl.at[:, 0, high], south_c, gx, north),
        (ctrl.at[:, 0, low], north_c, gx, south),
        (diff.at[:, 0, high], south_d, gx, north),
        (diff.at[:, 0, low], north_d, gx, south),
        (pack_e.at[high], w_ext.at[ext_low], east, north),
        (pack_e.at[low], w_ext.at[ext_high], east, south),
        (pack_w.at[high], e_ext.at[ext_low], west, north),
        (pack_w.at[low], e_ext.at[ext_high], west, south),
    )
    halo_copies = [
        pltpu.make_async_remote_copy(
            src_ref=src,
            dst_ref=dst,
            send_sem=halo_send.at[n],
            recv_sem=halo_recv.at[n],
            device_id={"gx": to_x, "gy": to_y, "obs": gz},
            device_id_type=MESH,
        )
        for n, (src, dst, to_x, to_y) in enumerate(routes)
    ]
    for copy in halo_copies:
        copy.start()

    def tile_copy(src, dst, send, recv, i, source):
        return pltpu.make_async_remote_copy(
            src_ref=src,
            dst_ref=dst.at[source],
            send_sem=send.at[i],
            recv_sem=recv.at[source],
            device_id=tile_device(other_tile(i)),
            device_id_type=MESH,
        )

    def level_copy(src, dst, send, recv, i, source):
        return pltpu.make_async_remote_copy(
            src_ref=src,
            dst_ref=dst.at[source],
            send_sem=send.at[i],
            recv_sem=recv.at[source],
            device_id=level_device(other_level(i)),
            device_id_type=MESH,
        )

    @pl.loop(1, tiles)
    def _(i):
        tile_copy(codes.at[me], codes, code_send, code_recv, i, me).start()

    for fetch in fetches[4:]:
        fetch.wait()

    profs, obs_count = codes.shape[2], oprof.shape[1]
    row_m = lax.broadcasted_iota(jnp.int32, (profs, obs_count), 0)
    match[...] = (row_m == oprof[...]).astype(jnp.float32).astype(jnp.bfloat16)
    slot = lax.broadcasted_iota(jnp.int32, (nz * fields, obs_count), 0)
    wanted = olevel[...] * fields + ofield[...]
    weight = oweight[...]
    mix[...] = jnp.where(slot == wanted, weight, jnp.where(slot == wanted + fields, 1.0 - weight, 0.0))

    for copy in halo_copies:
        copy.wait()

    lane_x = lax.broadcasted_iota(jnp.int32, (rows, LANES), 1)

    def aux_plane(j):
        from_east = e_ext[...] if j == 0 else pltpu.roll(e_ext[...], LANES - HALO * j, 1)
        from_west = pltpu.roll(w_ext[...], LANES - HALO * (j + 1), 1)
        rest = jnp.where(lane_x >= LANES - HALO, from_west, 0.0)
        return jnp.where(lane_x < HALO, from_east, rest)

    def put_plane(target, s, plane):
        target[pl.ds(s, rows, stride=GROUP), :] = plane

    for f in range(fields):
        field_a[pl.ds(f, HALO, stride=GROUP), :] = south_c[f]
        field_a[pl.ds(GROUP * HALO + f, cy, stride=GROUP), :] = ctrl[f, 0]
        field_a[pl.ds(GROUP * (HALO + cy) + f, HALO, stride=GROUP), :] = north_c[f]
        put_plane(field_a, fields + f, aux_plane(f))

    lat_count = ny * cy
    row_x = lax.broadcasted_iota(jnp.int32, (rows, LANES), 0) + (gy * cy - HALO)
    wall = (row_x == lat_count - 1) | (row_x == -1)

    def main_plane(k):
        return jnp.concatenate([south_d[k], diff[k, 0], north_d[k]], axis=0)

    e_main, e_aux = main_plane(0), aux_plane(fields)
    n_main = jnp.where(wall, 0.0, main_plane(1))
    n_aux = jnp.where(wall, 0.0, aux_plane(fields + 1))
    for target, main, aux in ((rate_e, e_main, e_aux), (rate_n, n_main, n_aux)):
        for f in range(fields):
            put_plane(target, f, main)
            put_plane(target, fields + f, aux)

    margin = HALO - STEPS + 1
    span = rows - 2 * margin
    size = span * GROUP
    here = pl.ds(margin * GROUP, size)
    before, after = pl.ds((margin - 1) * GROUP, size), pl.ds((margin + 1) * GROUP, size)
    lane_c = lax.broadcasted_iota(jnp.int32, (size, LANES), 1)

    def swap(v):
        return pltpu.roll(v.reshape(span, GROUP, LANES), fields, 1).reshape(size, LANES)

    def west_of(v, swapped):
        return pltpu.roll(jnp.where(lane_c == LANES - 1, swapped, v), 1, 1)

    e, n = rate_e[here, :], rate_n[here, :]
    w = west_of(e, swap(e))
    rate_w[here, :] = w
    rate_0[here, :] = 1.0 - (e + w + n + rate_n[before, :])

    def step(old, new):
        v = old[here, :]
        swapped = swap(v)
        v_east = pltpu.roll(jnp.where(lane_c == 0, swapped, v), LANES - 1, 1)
        new[here, :] = (
            rate_0[here, :] * v
            + rate_e[here, :] * v_east
            + rate_w[here, :] * west_of(v, swapped)
            + rate_n[here, :] * old[after, :]
            + rate_n[before, :] * old[before, :]
        )

    def diffuse():
        @pl.loop(0, STEPS // 2)
        def _(_):
            step(field_a, field_b)
            step(field_b, field_a)

    diffuse()

    for f in range(fields):
        turned = field_a[pl.ds(GROUP * HALO + f, cy, stride=GROUP), :].T
        big, small = two_parts(turned)
        gather_lhs[pl.ds(f * cx, cx), 0:cy] = big.astype(jnp.bfloat16)
        gather_lhs[pl.ds(f * cx, cx), cy : 2 * cy] = small.astype(jnp.bfloat16)

    row_p = lax.broadcasted_iota(jnp.int32, (cy, profs), 0)

    def gather_for(tile):
        holder, cell = codes[tile, 0:1], codes[tile, 1:2]
        y, x = halves(cell, cx)
        y = jnp.where(holder == me, y, -1)
        pick = (row_p == y).astype(jnp.float32).astype(jnp.bfloat16)
        found = jnp.dot(
            gather_lhs[...],
            jnp.concatenate([pick, pick], axis=0),
            preferred_element_type=jnp.float32,
        )
        column = row_p == x
        sums = [
            jnp.sum(jnp.where(column, found[f * cx : (f + 1) * cx], 0.0), axis=0, keepdims=True)
            for f in range(fields)
        ]
        return jnp.concatenate(sums, axis=0)

    @pl.loop(1, tiles)
    def _(i):
        tile = other_tile(i)
        copy = tile_copy(codes.at[tile], codes, code_send, code_recv, i, tile)
        copy.wait_recv()
        gathered[i] = gather_for(tile)
        tile_copy(gathered.at[i], col_in, col_send, col_recv, i, me).start()

    col_in[me] = gather_for(me)

    total = col_in[me]
    gathered[0] = total

    @pl.loop(1, tiles)
    def _(i):
        tile = other_tile(i)
        tile_copy(gathered.at[i], col_in, col_send, col_recv, i, tile).wait_recv()
        gathered[0] = gathered[0] + col_in[tile]

    col_all[gz] = gathered[0]

    @pl.loop(1, nz)
    def _(i):
        level_copy(col_all.at[gz], col_all, lev_send, lev_recv, i, gz).start()

    row_r = lax.broadcasted_iota(jnp.int32, (rows, profs), 0)
    row_c = lax.broadcasted_iota(jnp.int32, (2 * LANES, profs), 0)

    @pl.loop(0, tiles)
    def _(tile):
        holder, cell = codes[tile, 0:1], codes[tile, 1:2]
        holder_x, _ = halves(holder, ny)
        _, x = halves(cell, cx)
        side = ((holder_x == east) & (x < cx // 2)) | ((holder_x == west) & (x >= cx // 2))
        place = jnp.where(holder_x == gx, x, jnp.where(side, LANES + x, -1))
        spots[tile] = (row_c == place).astype(jnp.float32).astype(jnp.bfloat16)

    @pl.loop(1, nz)
    def _(i):
        level = other_level(i)
        level_copy(col_all.at[level], col_all, lev_send, lev_recv, i, level).wait_recv()

    wide = nz * fields
    big, small = two_parts(col_all[...].reshape(wide, profs))
    both = jnp.concatenate([big, small], axis=0).astype(jnp.bfloat16)
    seen = jnp.dot(both, match[...], preferred_element_type=jnp.float32)
    seen = seen[0:wide] + seen[wide:]
    observed = jnp.sum(mix[...] * seen, axis=0, keepdims=True)
    departures = oprec[...] * (observed - innov[...])
    dep_out[...] = departures
    big, small = two_parts(mix[...] * departures)
    both = jnp.concatenate([big, small], axis=0).astype(jnp.bfloat16)
    back = lax.dot_general(
        both, match[...], (((1,), (1,)), ((), ())), preferred_element_type=jnp.float32
    )
    adj_part[...] = (back[0:wide] + back[wide:]).reshape(nz, fields, profs)

    @pl.loop(1, nz)
    def _(i):
        level_copy(adj_part.at[other_level(i)], adj_in, red_send, red_recv, i, gz).start()

    @pl.loop(0, tiles)
    def _(tile):
        holder, cell = codes[tile, 0:1], codes[tile, 1:2]
        _, holder_y = halves(holder, ny)
        y, _ = halves(cell, cx)
        near = row_r == (holder_y - gy) * cy + y + HALO
        nears[tile] = near.astype(jnp.float32).astype(jnp.bfloat16)

    gathered[0] = adj_part[gz]

    @pl.loop(1, nz)
    def _(i):
        level = other_level(i)
        level_copy(adj_part.at[level], adj_in, red_send, red_recv, i, level).wait_recv()
        gathered[0] = gathered[0] + adj_in[level]

    adj_all[me] = gathered[0]

    @pl.loop(1, tiles)
    def _(i):
        tile_copy(adj_all.at[me], adj_all, adj_send, adj_recv, i, me).start()

    def scatter_from(tile):
        big, small = (part.astype(jnp.bfloat16) for part in two_parts(adj_all[tile]))
        near = nears[tile]
        lines = [
            jnp.concatenate([near * big[f : f + 1], near * small[f : f + 1]], axis=1)
            for f in range(fields)
        ]
        spot = spots[tile]
        return lax.dot_general(
            jnp.concatenate(lines, axis=0),
            jnp.concatenate([spot, spot], axis=1),
            (((1,), (1,)), ((), ())),
            preferred_element_type=jnp.float32,
        )

    spread[...] = scatter_from(me)

    @pl.loop(1, tiles)
    def _(i):
        tile = other_tile(i)
        tile_copy(adj_all.at[me], adj_all, adj_send, adj_recv, i, tile).wait_recv()
        spread[...] += scatter_from(tile)

    for f in range(fields):
        put_plane(field_a, f, spread[pl.ds(f * rows, rows), 0:LANES])
        put_plane(field_a, fields + f, spread[pl.ds(f * rows, rows), LANES : 2 * LANES])

    diffuse()

    for f in range(fields):
        grad_out[f, 0] = field_a[pl.ds(GROUP * HALO + f, cy, stride=GROUP), :]

    @pl.loop(1, tiles)
    def _(i):
        tile_copy(codes.at[me], codes, code_send, code_recv, i, me).wait_send()
        tile_copy(gathered.at[i], col_in, col_send, col_recv, i, me).wait_send()
        tile_copy(adj_all.at[me], adj_all, adj_send, adj_recv, i, me).wait_send()

    @pl.loop(1, nz)
    def _(i):
        level_copy(col_all.at[gz], col_all, lev_send, lev_recv, i, gz).wait_send()
        level_copy(adj_part.at[other_level(i)], adj_in, red_send, red_recv, i, gz).wait_send()


def per_device(
    nx, ny, nz,
    control,
    diffusivity,
    prof_tile,
    prof_cell,
    obs_prof,
    obs_field,
    obs_level,
    obs_weight,
    innovation,
    obs_precision,
):
    fields, _, cy, cx = control.shape
    profs = prof_cell.shape[0]
    obs_count = obs_prof.shape[0]
    tiles = nx * ny
    rows = cy + 2 * HALO
    f32 = jnp.float32

    def plane(*shape):
        return pltpu.VMEM(shape, f32)

    def flags(count):
        return pltpu.SemaphoreType.DMA((count,))

    def numbers(count):
        return pltpu.VMEM((1, count), jnp.int32)

    scratch = [
        plane(*control.shape), plane(*diffusivity.shape), numbers(profs), numbers(profs),
        numbers(obs_count), numbers(obs_count), numbers(obs_count),
        plane(1, obs_count), plane(1, obs_count), plane(1, obs_count), flags(10),
        pltpu.VMEM((profs, obs_count), jnp.bfloat16), plane(nz * fields, obs_count),
    ]
    scratch += [
        plane(cy, LANES), plane(cy, LANES), plane(rows, LANES), plane(rows, LANES),
        plane(fields, HALO, LANES), plane(fields, HALO, LANES),
        plane(2, HALO, LANES), plane(2, HALO, LANES),
        pltpu.VMEM((tiles, 2, profs), jnp.int32),
    ]
    scratch += [plane(rows * GROUP, LANES)] * 6
    scratch += [
        pltpu.VMEM((fields * cx, 2 * cy), jnp.bfloat16),
        plane(tiles, fields, profs),
        plane(tiles, fields, profs),
        plane(nz, fields, profs),
        plane(nz, fields, profs),
        plane(nz, fields, profs),
        plane(tiles, fields, profs),
        plane(fields * rows, 2 * LANES),
        pltpu.VMEM((tiles, 2 * LANES, profs), jnp.bfloat16),
        pltpu.VMEM((tiles, rows, profs), jnp.bfloat16),
        flags(10), flags(10),
        flags(tiles), flags(tiles), flags(tiles), flags(tiles),
        flags(nz), flags(nz), flags(nz), flags(nz),
        flags(tiles), flags(tiles),
    ]
    spread, departures = pl.pallas_call(
        functools.partial(kernel, nx, ny, nz),
        out_shape=(
            jax.ShapeDtypeStruct(control.shape, f32),
            jax.ShapeDtypeStruct((1, obs_count), f32),
        ),
        in_specs=[pl.BlockSpec(memory_space=pltpu.HBM)] * 10,
        out_specs=(pl.BlockSpec(memory_space=pltpu.VMEM),) * 2,
        scratch_shapes=scratch,
        compiler_params=pltpu.CompilerParams(
            collective_id=0, has_side_effects=True, vmem_limit_bytes=64 * 1024 * 1024
        ),
    )(
        control,
        diffusivity,
        prof_tile.reshape(1, profs),
        prof_cell.reshape(1, profs),
        obs_prof.reshape(1, obs_count),
        obs_field.reshape(1, obs_count),
        obs_level.reshape(1, obs_count),
        obs_weight.reshape(1, obs_count),
        innovation.reshape(1, obs_count),
        obs_precision.reshape(1, obs_count),
    )
    return (control + spread, departures.reshape(obs_count))


def solution(mesh):
    nx, ny, nz = mesh.shape["gx"], mesh.shape["gy"], mesh.shape["obs"]
    in_specs = (
        P(None, "obs", "gy", "gx"),
        P(None, "obs", "gy", "gx"),
        P(("gx", "gy"), None),
        P(("gx", "gy")),
        P(("gx", "gy", "obs")),
        P(("gx", "gy", "obs")),
        P(("gx", "gy", "obs")),
        P(("gx", "gy", "obs")),
        P(("gx", "gy", "obs")),
        P(("gx", "gy", "obs")),
    )
    out_specs = (P(None, "obs", "gy", "gx"), P(("gx", "gy", "obs")))
    return jax.shard_map(
        functools.partial(per_device, nx, ny, nz),
        mesh=mesh,
        in_specs=in_specs,
        out_specs=out_specs,
        check_vma=False,
    )
```

```python
import functools

import jax
import jax.numpy as jnp
from jax import lax
from jax.experimental import pallas as pl
from jax.experimental.pallas import tpu as pltpu
from jax.sharding import PartitionSpec as P

STEPS = 10
HALO = 16
LANES = 128
GROUP = 8
BLOCK = 15
MESH = pl.DeviceIdType.MESH


def halves(value, size):
    if size & (size - 1) == 0:
        return value >> (size.bit_length() - 1), value & (size - 1)
    return value // size, value % size


def two_parts(value):
    high = value.astype(jnp.bfloat16).astype(jnp.float32)
    return high, value - high


def kernel(
    nx, ny, nz,
    ctrl_in, diff_in, ptile_in, pcell_in, oprof_in, ofield_in, olevel_in, oweight_in, innov_in, oprec_in,
    grad_out, dep_out,
    ctrl, diff, ptile, pcell, oprof, ofield, olevel, oweight, innov, oprec, fetched, match, mix,
    pack_e, pack_w, w_ext, e_ext, south_c, north_c, south_d, north_d,
    codes, field_a, field_b, rate_e, rate_w, rate_n, rate_0,
    gather_lhs, gathered, col_in, col_all, adj_part, adj_in, adj_all, spread, spots, nears,
    halo_send, halo_recv, code_send, code_recv, col_send, col_recv,
    lev_send, lev_recv, red_send, red_recv, adj_send, adj_recv,
):
    fields, _, cy, cx = ctrl.shape
    tiles = nx * ny
    rows = cy + 2 * HALO
    gx, gy, gz = lax.axis_index("gx"), lax.axis_index("gy"), lax.axis_index("obs")
    me = gx * ny + gy
    east, west = lax.rem(gx + 1, nx), lax.rem(gx + nx - 1, nx)
    north, south = lax.rem(gy + 1, ny), lax.rem(gy + ny - 1, ny)

    def tile_device(tile):
        return {"gx": lax.div(tile, ny), "gy": lax.rem(tile, ny), "obs": gz}

    def level_device(level):
        return {"gx": gx, "gy": gy, "obs": level}

    def other_tile(i):
        return lax.rem(me + i, tiles)

    def other_level(i):
        return lax.rem(gz + i, nz)

    fetches = [
        pltpu.make_async_copy(src, dst, fetched.at[n])
        for n, (src, dst) in enumerate((
            (ctrl_in, ctrl), (diff_in, diff), (ptile_in, ptile), (pcell_in, pcell),
            (oprof_in, oprof), (ofield_in, ofield), (olevel_in, olevel),
            (oweight_in, oweight), (innov_in, innov), (oprec_in, oprec),
        ))
    ]
    for fetch in fetches:
        fetch.start()

    barrier = pltpu.get_barrier_semaphore()

    @pl.loop(1, tiles)
    def _(i):
        pl.semaphore_signal(barrier, inc=1, device_id=tile_device(other_tile(i)), device_id_type=MESH)

    @pl.loop(1, nz)
    def _(i):
        pl.semaphore_signal(barrier, inc=1, device_id=level_device(other_level(i)), device_id_type=MESH)

    for fetch in fetches[0:4]:
        fetch.wait()

    lane = lax.broadcasted_iota(jnp.int32, (cy, LANES), 1)
    first = jnp.zeros((cy, LANES), jnp.float32)
    last = jnp.zeros((cy, LANES), jnp.float32)
    for j in range(fields + 2):
        plane = ctrl[j, 0] if j < fields else diff[j - fields, 0]
        here = (lane >= HALO * j) & (lane < HALO * (j + 1))
        last = jnp.where(here, pltpu.roll(plane, (HALO * (j + 1)) % LANES, 1), last)
        moved = plane if j == 0 else pltpu.roll(plane, HALO * j, 1)
        first = jnp.where(here, moved, first)
    pack_e[...] = last
    pack_w[...] = first
    codes[me, 0:1] = ptile[...]
    codes[me, 1:2] = pcell[...]

    pl.semaphore_wait(barrier, tiles - 1 + nz - 1)

    low, high = pl.ds(0, HALO), pl.ds(cy - HALO, HALO)
    ext_low, ext_mid, ext_high = pl.ds(0, HALO), pl.ds(HALO, cy), pl.ds(HALO + cy, HALO)
    routes = (
        (pack_e, w_ext.at[ext_mid], east, gy),
        (pack_w, e_ext.at[ext_mid], west, gy),
        (ctrl.at[:, 0, high], south_c, gx, north),
        (ctrl.at[:, 0, low], north_c, gx, south),
        (diff.at[:, 0, high], south_d, gx, north),
        (diff.at[:, 0, low], north_d, gx, south),
        (pack_e.at[high], w_ext.at[ext_low], east, north),
        (pack_e.at[low], w_ext.at[ext_high], east, south),
        (pack_w.at[high], e_ext.at[ext_low], west, north),
        (pack_w.at[low], e_ext.at[ext_high], west, south),
    )
    halo_copies = [
        pltpu.make_async_remote_copy(
            src_ref=src,
            dst_ref=dst,
            send_sem=halo_send.at[n],
            recv_sem=halo_recv.at[n],
            device_id={"gx": to_x, "gy": to_y, "obs": gz},
            device_id_type=MESH,
        )
        for n, (src, dst, to_x, to_y) in enumerate(routes)
    ]
    for copy in halo_copies:
        copy.start()

    def tile_copy(src, dst, send, recv, i, source):
        return pltpu.make_async_remote_copy(
            src_ref=src,
            dst_ref=dst.at[source],
            send_sem=send.at[i],
            recv_sem=recv.at[source],
            device_id=tile_device(other_tile(i)),
            device_id_type=MESH,
        )

    def level_copy(src, dst, send, recv, i, source):
        return pltpu.make_async_remote_copy(
            src_ref=src,
            dst_ref=dst.at[source],
            send_sem=send.at[i],
            recv_sem=recv.at[source],
            device_id=level_device(other_level(i)),
            device_id_type=MESH,
        )

    @pl.loop(1, tiles)
    def _(i):
        tile_copy(codes.at[me], codes, code_send, code_recv, i, me).start()

    for fetch in fetches[4:]:
        fetch.wait()

    profs, obs_count = codes.shape[2], oprof.shape[1]
    row_m = lax.broadcasted_iota(jnp.int32, (profs, obs_count), 0)
    match[...] = (row_m == oprof[...]).astype(jnp.float32).astype(jnp.bfloat16)
    slot = lax.broadcasted_iota(jnp.int32, (nz * fields, obs_count), 0)
    wanted = olevel[...] * fields + ofield[...]
    weight = oweight[...]
    mix[...] = jnp.where(slot == wanted, weight, jnp.where(slot == wanted + fields, 1.0 - weight, 0.0))

    def put_plane(target, s, plane, start=0):
        target[pl.ds(GROUP * start + s, plane.shape[0], stride=GROUP), :] = plane

    lat_count = ny * cy
    row_y = lax.broadcasted_iota(jnp.int32, (cy, LANES), 0) + gy * cy
    n_own = jnp.where(row_y == lat_count - 1, 0.0, diff[1, 0])
    for f in range(fields):
        put_plane(field_a, f, ctrl[f, 0], HALO)
        put_plane(rate_e, f, diff[0, 0], HALO)
        put_plane(rate_n, f, n_own, HALO)

    for copy in halo_copies:
        copy.wait()

    lane_x = lax.broadcasted_iota(jnp.int32, (rows, LANES), 1)

    def aux_plane(j):
        from_east = e_ext[...] if j == 0 else pltpu.roll(e_ext[...], LANES - HALO * j, 1)
        from_west = pltpu.roll(w_ext[...], LANES - HALO * (j + 1), 1)
        rest = jnp.where(lane_x >= LANES - HALO, from_west, 0.0)
        return jnp.where(lane_x < HALO, from_east, rest)

    row_x = lax.broadcasted_iota(jnp.int32, (rows, LANES), 0) + (gy * cy - HALO)
    wall = (row_x == lat_count - 1) | (row_x == -1)
    row_s = lax.broadcasted_iota(jnp.int32, (HALO, LANES), 0) + (gy * cy - HALO)
    e_aux = aux_plane(fields)
    n_aux = jnp.where(wall, 0.0, aux_plane(fields + 1))
    n_south = jnp.where(row_s == -1, 0.0, south_d[1])
    for f in range(fields):
        put_plane(field_a, f, south_c[f])
        put_plane(field_a, f, north_c[f], HALO + cy)
        put_plane(field_a, fields + f, aux_plane(f))
        put_plane(rate_e, f, south_d[0])
        put_plane(rate_e, f, north_d[0], HALO + cy)
        put_plane(rate_e, fields + f, e_aux)
        put_plane(rate_n, f, n_south)
        put_plane(rate_n, f, north_d[1], HALO + cy)
        put_plane(rate_n, fields + f, n_aux)

    margin = HALO - STEPS + 1
    span = rows - 2 * margin
    count = -(-span // BLOCK)
    edges = [margin + span * k // count for k in range(count + 1)]

    def swap(v):
        return pltpu.roll(v.reshape(-1, GROUP, LANES), fields, 1).reshape(v.shape)

    def lanes_of(v):
        return lax.broadcasted_iota(jnp.int32, v.shape, 1)

    def west_of(v, swapped):
        return pltpu.roll(jnp.where(lanes_of(v) == LANES - 1, swapped, v), 1, 1)

    for low_row, high_row in zip(edges[:-1], edges[1:]):
        size = (high_row - low_row) * GROUP
        here = pl.ds(low_row * GROUP, size)
        e = rate_e[here, :]
        n = rate_n[pl.ds((low_row - 1) * GROUP, size + GROUP), :]
        w = west_of(e, swap(e))
        rate_w[here, :] = w
        rate_0[here, :] = 1.0 - (e + w + n[GROUP:] + n[:-GROUP])

    def step(old, new):
        for low_row, high_row in zip(edges[:-1], edges[1:]):
            size = (high_row - low_row) * GROUP
            here = pl.ds(low_row * GROUP, size)
            n = rate_n[pl.ds((low_row - 1) * GROUP, size + GROUP), :]
            tall = old[pl.ds((low_row - 1) * GROUP, size + 2 * GROUP), :]
            v = tall[GROUP:-GROUP]
            swapped = swap(v)
            v_east = pltpu.roll(jnp.where(lanes_of(v) == 0, swapped, v), LANES - 1, 1)
            new[here, :] = (
                rate_0[here, :] * v
                + rate_e[here, :] * v_east
                + rate_w[here, :] * west_of(v, swapped)
                + n[GROUP:] * tall[2 * GROUP :]
                + n[:-GROUP] * tall[: -2 * GROUP]
            )

    def diffuse():
        @pl.loop(0, STEPS // 2)
        def _(_):
            step(field_a, field_b)
            step(field_b, field_a)

    diffuse()

    for f in range(fields):
        turned = field_a[pl.ds(GROUP * HALO + f, cy, stride=GROUP), :].T
        big, small = two_parts(turned)
        gather_lhs[pl.ds(f * cx, cx), 0:cy] = big.astype(jnp.bfloat16)
        gather_lhs[pl.ds(f * cx, cx), cy : 2 * cy] = small.astype(jnp.bfloat16)

    row_p = lax.broadcasted_iota(jnp.int32, (cy, profs), 0)

    def gather_for(tile):
        holder, cell = codes[tile, 0:1], codes[tile, 1:2]
        y, x = halves(cell, cx)
        y = jnp.where(holder == me, y, -1)
        pick = (row_p == y).astype(jnp.float32).astype(jnp.bfloat16)
        found = jnp.dot(
            gather_lhs[...],
            jnp.concatenate([pick, pick], axis=0),
            preferred_element_type=jnp.float32,
        )
        column = row_p == x
        sums = [
            jnp.sum(jnp.where(column, found[f * cx : (f + 1) * cx], 0.0), axis=0, keepdims=True)
            for f in range(fields)
        ]
        return jnp.concatenate(sums, axis=0)

    @pl.loop(1, tiles)
    def _(i):
        tile = other_tile(i)
        tile_copy(codes.at[tile], codes, code_send, code_recv, i, tile).wait_recv()

    together = 4 if tiles % 4 == 0 else 1

    @pl.loop(0, tiles // together)
    def _(g):
        for k in range(together):
            i = lax.rem(g * together + k + 1, tiles)
            gathered[i] = gather_for(other_tile(i))
        for k in range(together):
            i = g * together + k + 1

            @pl.when(i < tiles)
            def _():
                tile_copy(gathered.at[i], col_in, col_send, col_recv, i, me).start()

    @pl.loop(1, tiles)
    def _(i):
        tile = other_tile(i)
        tile_copy(gathered.at[i], col_in, col_send, col_recv, i, tile).wait_recv()
        gathered[0] = gathered[0] + col_in[tile]

    col_all[gz] = gathered[0]

    @pl.loop(1, nz)
    def _(i):
        level_copy(col_all.at[gz], col_all, lev_send, lev_recv, i, gz).start()

    row_r = lax.broadcasted_iota(jnp.int32, (rows, profs), 0)
    row_c = lax.broadcasted_iota(jnp.int32, (2 * LANES, profs), 0)

    @pl.loop(0, tiles)
    def _(tile):
        holder, cell = codes[tile, 0:1], codes[tile, 1:2]
        holder_x, _ = halves(holder, ny)
        _, x = halves(cell, cx)
        side = ((holder_x == east) & (x < cx // 2)) | ((holder_x == west) & (x >= cx // 2))
        place = jnp.where(holder_x == gx, x, jnp.where(side, LANES + x, -1))
        spots[tile] = (row_c == place).astype(jnp.float32).astype(jnp.bfloat16)

    @pl.loop(1, nz)
    def _(i):
        level = other_level(i)
        level_copy(col_all.at[level], col_all, lev_send, lev_recv, i, level).wait_recv()

    wide = nz * fields
    big, small = two_parts(col_all[...].reshape(wide, profs))
    both = jnp.concatenate([big, small], axis=0).astype(jnp.bfloat16)
    seen = jnp.dot(both, match[...], preferred_element_type=jnp.float32)
    seen = seen[0:wide] + seen[wide:]
    observed = jnp.sum(mix[...] * seen, axis=0, keepdims=True)
    departures = oprec[...] * (observed - innov[...])
    dep_out[...] = departures
    big, small = two_parts(mix[...] * departures)
    both = jnp.concatenate([big, small], axis=0).astype(jnp.bfloat16)
    back = lax.dot_general(
        both, match[...], (((1,), (1,)), ((), ())), preferred_element_type=jnp.float32
    )
    adj_part[...] = (back[0:wide] + back[wide:]).reshape(nz, fields, profs)

    @pl.loop(1, nz)
    def _(i):
        level_copy(adj_part.at[other_level(i)], adj_in, red_send, red_recv, i, gz).start()

    @pl.loop(0, tiles)
    def _(tile):
        holder, cell = codes[tile, 0:1], codes[tile, 1:2]
        _, holder_y = halves(holder, ny)
        y, _ = halves(cell, cx)
        near = row_r == (holder_y - gy) * cy + y + HALO
        nears[tile] = near.astype(jnp.float32).astype(jnp.bfloat16)

    gathered[0] = adj_part[gz]

    @pl.loop(1, nz)
    def _(i):
        level = other_level(i)
        level_copy(adj_part.at[level], adj_in, red_send, red_recv, i, level).wait_recv()
        gathered[0] = gathered[0] + adj_in[level]

    adj_all[me] = gathered[0]

    @pl.loop(1, tiles)
    def _(i):
        tile_copy(adj_all.at[me], adj_all, adj_send, adj_recv, i, me).start()

    def scatter_from(some):
        lines = [[] for _ in range(fields)]
        places = []
        for tile in some:
            near = nears[tile]
            for part in two_parts(adj_all[tile]):
                part = part.astype(jnp.bfloat16)
                places.append(spots[tile])
                for f in range(fields):
                    lines[f].append(near * part[f : f + 1])
        return lax.dot_general(
            jnp.concatenate([jnp.concatenate(line, axis=1) for line in lines], axis=0),
            jnp.concatenate(places, axis=1),
            (((1,), (1,)), ((), ())),
            preferred_element_type=jnp.float32,
        )

    spread[...] = scatter_from([me])
    joined = 7 if (tiles - 1) % 7 == 0 else 1

    @pl.loop(0, (tiles - 1) // joined)
    def _(g):
        some = [other_tile(g * joined + k + 1) for k in range(joined)]
        for k, tile in enumerate(some):
            i = g * joined + k + 1
            tile_copy(adj_all.at[me], adj_all, adj_send, adj_recv, i, tile).wait_recv()
        spread[...] += scatter_from(some)

    for f in range(fields):
        put_plane(field_a, f, spread[pl.ds(f * rows, rows), 0:LANES])
        put_plane(field_a, fields + f, spread[pl.ds(f * rows, rows), LANES : 2 * LANES])

    diffuse()

    for f in range(fields):
        grad_out[f, 0] = field_a[pl.ds(GROUP * HALO + f, cy, stride=GROUP), :]

    @pl.loop(1, tiles)
    def _(i):
        tile_copy(codes.at[me], codes, code_send, code_recv, i, me).wait_send()
        tile_copy(gathered.at[i], col_in, col_send, col_recv, i, me).wait_send()
        tile_copy(adj_all.at[me], adj_all, adj_send, adj_recv, i, me).wait_send()

    @pl.loop(1, nz)
    def _(i):
        level_copy(col_all.at[gz], col_all, lev_send, lev_recv, i, gz).wait_send()
        level_copy(adj_part.at[other_level(i)], adj_in, red_send, red_recv, i, gz).wait_send()


def per_device(
    nx, ny, nz,
    control,
    diffusivity,
    prof_tile,
    prof_cell,
    obs_prof,
    obs_field,
    obs_level,
    obs_weight,
    innovation,
    obs_precision,
):
    fields, _, cy, cx = control.shape
    profs = prof_cell.shape[0]
    obs_count = obs_prof.shape[0]
    tiles = nx * ny
    rows = cy + 2 * HALO
    f32 = jnp.float32

    def plane(*shape):
        return pltpu.VMEM(shape, f32)

    def flags(count):
        return pltpu.SemaphoreType.DMA((count,))

    def numbers(count):
        return pltpu.VMEM((1, count), jnp.int32)

    scratch = [
        plane(*control.shape), plane(*diffusivity.shape), numbers(profs), numbers(profs),
        numbers(obs_count), numbers(obs_count), numbers(obs_count),
        plane(1, obs_count), plane(1, obs_count), plane(1, obs_count), flags(10),
        pltpu.VMEM((profs, obs_count), jnp.bfloat16), plane(nz * fields, obs_count),
    ]
    scratch += [
        plane(cy, LANES), plane(cy, LANES), plane(rows, LANES), plane(rows, LANES),
        plane(fields, HALO, LANES), plane(fields, HALO, LANES),
        plane(2, HALO, LANES), plane(2, HALO, LANES),
        pltpu.VMEM((tiles, 2, profs), jnp.int32),
    ]
    scratch += [plane(rows * GROUP, LANES)] * 6
    scratch += [
        pltpu.VMEM((fields * cx, 2 * cy), jnp.bfloat16),
        plane(tiles, fields, profs),
        plane(tiles, fields, profs),
        plane(nz, fields, profs),
        plane(nz, fields, profs),
        plane(nz, fields, profs),
        plane(tiles, fields, profs),
        plane(fields * rows, 2 * LANES),
        pltpu.VMEM((tiles, 2 * LANES, profs), jnp.bfloat16),
        pltpu.VMEM((tiles, rows, profs), jnp.bfloat16),
        flags(10), flags(10),
        flags(tiles), flags(tiles), flags(tiles), flags(tiles),
        flags(nz), flags(nz), flags(nz), flags(nz),
        flags(tiles), flags(tiles),
    ]
    spread, departures = pl.pallas_call(
        functools.partial(kernel, nx, ny, nz),
        out_shape=(
            jax.ShapeDtypeStruct(control.shape, f32),
            jax.ShapeDtypeStruct((1, obs_count), f32),
        ),
        in_specs=[pl.BlockSpec(memory_space=pltpu.HBM)] * 10,
        out_specs=(pl.BlockSpec(memory_space=pltpu.VMEM),) * 2,
        scratch_shapes=scratch,
        compiler_params=pltpu.CompilerParams(
            collective_id=0, has_side_effects=True, vmem_limit_bytes=64 * 1024 * 1024
        ),
    )(
        control,
        diffusivity,
        prof_tile.reshape(1, profs),
        prof_cell.reshape(1, profs),
        obs_prof.reshape(1, obs_count),
        obs_field.reshape(1, obs_count),
        obs_level.reshape(1, obs_count),
        obs_weight.reshape(1, obs_count),
        innovation.reshape(1, obs_count),
        obs_precision.reshape(1, obs_count),
    )
    return (control + spread, departures.reshape(obs_count))


def solution(mesh):
    nx, ny, nz = mesh.shape["gx"], mesh.shape["gy"], mesh.shape["obs"]
    in_specs = (
        P(None, "obs", "gy", "gx"),
        P(None, "obs", "gy", "gx"),
        P(("gx", "gy"), None),
        P(("gx", "gy")),
        P(("gx", "gy", "obs")),
        P(("gx", "gy", "obs")),
        P(("gx", "gy", "obs")),
        P(("gx", "gy", "obs")),
        P(("gx", "gy", "obs")),
        P(("gx", "gy", "obs")),
    )
    out_specs = (P(None, "obs", "gy", "gx"), P(("gx", "gy", "obs")))
    return jax.shard_map(
        functools.partial(per_device, nx, ny, nz),
        mesh=mesh,
        in_specs=in_specs,
        out_specs=out_specs,
        check_vma=False,
    )
```

```python
import functools

import jax
import jax.numpy as jnp
from jax import lax
from jax.experimental import pallas as pl
from jax.experimental.pallas import tpu as pltpu
from jax.sharding import PartitionSpec as P

STEPS = 10
HALO = 16
LANES = 128
GROUP = 8
BLOCK = 15
MESH = pl.DeviceIdType.MESH


def halves(value, size):
    if size & (size - 1) == 0:
        return value >> (size.bit_length() - 1), value & (size - 1)
    return value // size, value % size


def two_parts(value):
    high = value.astype(jnp.bfloat16).astype(jnp.float32)
    return high, value - high


def kernel(
    nx, ny, nz,
    ctrl_in, diff_in, ptile_in, pcell_in, oprof_in, ofield_in, olevel_in, oweight_in, innov_in, oprec_in,
    grad_out, dep_out,
    ctrl, diff, ptile, pcell, oprof, ofield, olevel, oweight, innov, oprec, fetched, match, mix,
    pack_e, pack_w, w_ext, e_ext, south_c, north_c, south_d, north_d,
    codes, field_a, field_b, rate_e, rate_w, rate_n, rate_0,
    gather_lhs, gathered, col_in, col_all, adj_part, adj_in, adj_all, spread, spots, nears,
    halo_send, halo_recv, code_send, code_recv, col_send, col_recv,
    lev_send, lev_recv, red_send, red_recv, adj_send, adj_recv,
):
    fields, _, cy, cx = ctrl.shape
    tiles = nx * ny
    rows = cy + 2 * HALO
    gx, gy, gz = lax.axis_index("gx"), lax.axis_index("gy"), lax.axis_index("obs")
    me = gx * ny + gy
    east, west = lax.rem(gx + 1, nx), lax.rem(gx + nx - 1, nx)
    north, south = lax.rem(gy + 1, ny), lax.rem(gy + ny - 1, ny)

    def tile_device(tile):
        return {"gx": lax.div(tile, ny), "gy": lax.rem(tile, ny), "obs": gz}

    def level_device(level):
        return {"gx": gx, "gy": gy, "obs": level}

    def other_tile(i):
        return lax.rem(me + i, tiles)

    def other_level(i):
        return lax.rem(gz + i, nz)

    fetches = [
        pltpu.make_async_copy(src, dst, fetched.at[n])
        for n, (src, dst) in enumerate((
            (ctrl_in, ctrl), (diff_in, diff), (ptile_in, ptile), (pcell_in, pcell),
            (oprof_in, oprof), (ofield_in, ofield), (olevel_in, olevel),
            (oweight_in, oweight), (innov_in, innov), (oprec_in, oprec),
        ))
    ]
    for fetch in fetches:
        fetch.start()

    barrier = pltpu.get_barrier_semaphore()

    @pl.loop(1, tiles)
    def _(i):
        pl.semaphore_signal(barrier, inc=1, device_id=tile_device(other_tile(i)), device_id_type=MESH)

    @pl.loop(1, nz)
    def _(i):
        pl.semaphore_signal(barrier, inc=1, device_id=level_device(other_level(i)), device_id_type=MESH)

    for fetch in fetches[0:4]:
        fetch.wait()

    lane = lax.broadcasted_iota(jnp.int32, (cy, LANES), 1)
    first = jnp.zeros((cy, LANES), jnp.float32)
    last = jnp.zeros((cy, LANES), jnp.float32)
    for j in range(fields + 2):
        plane = ctrl[j, 0] if j < fields else diff[j - fields, 0]
        here = (lane >= HALO * j) & (lane < HALO * (j + 1))
        last = jnp.where(here, pltpu.roll(plane, (HALO * (j + 1)) % LANES, 1), last)
        moved = plane if j == 0 else pltpu.roll(plane, HALO * j, 1)
        first = jnp.where(here, moved, first)
    pack_e[...] = last
    pack_w[...] = first
    codes[me, 0:1] = ptile[...]
    codes[me, 1:2] = pcell[...]

    pl.semaphore_wait(barrier, tiles - 1 + nz - 1)

    low, high = pl.ds(0, HALO), pl.ds(cy - HALO, HALO)
    ext_low, ext_mid, ext_high = pl.ds(0, HALO), pl.ds(HALO, cy), pl.ds(HALO + cy, HALO)
    routes = (
        (pack_e, w_ext.at[ext_mid], east, gy),
        (pack_w, e_ext.at[ext_mid], west, gy),
        (ctrl.at[:, 0, high], south_c, gx, north),
        (ctrl.at[:, 0, low], north_c, gx, south),
        (diff.at[:, 0, high], south_d, gx, north),
        (diff.at[:, 0, low], north_d, gx, south),
        (pack_e.at[high], w_ext.at[ext_low], east, north),
        (pack_e.at[low], w_ext.at[ext_high], east, south),
        (pack_w.at[high], e_ext.at[ext_low], west, north),
        (pack_w.at[low], e_ext.at[ext_high], west, south),
    )
    halo_copies = [
        pltpu.make_async_remote_copy(
            src_ref=src,
            dst_ref=dst,
            send_sem=halo_send.at[n],
            recv_sem=halo_recv.at[n],
            device_id={"gx": to_x, "gy": to_y, "obs": gz},
            device_id_type=MESH,
        )
        for n, (src, dst, to_x, to_y) in enumerate(routes)
    ]
    for copy in halo_copies:
        copy.start()

    def tile_copy(src, dst, send, recv, i, source):
        return pltpu.make_async_remote_copy(
            src_ref=src,
            dst_ref=dst.at[source],
            send_sem=send.at[i],
            recv_sem=recv.at[source],
            device_id=tile_device(other_tile(i)),
            device_id_type=MESH,
        )

    def level_copy(src, dst, send, recv, i, source):
        return pltpu.make_async_remote_copy(
            src_ref=src,
            dst_ref=dst.at[source],
            send_sem=send.at[i],
            recv_sem=recv.at[source],
            device_id=level_device(other_level(i)),
            device_id_type=MESH,
        )

    @pl.loop(1, tiles)
    def _(i):
        tile_copy(codes.at[me], codes, code_send, code_recv, i, me).start()

    for fetch in fetches[4:]:
        fetch.wait()

    profs, obs_count = codes.shape[2], oprof.shape[1]
    row_m = lax.broadcasted_iota(jnp.int32, (profs, obs_count), 0)
    match[...] = (row_m == oprof[...]).astype(jnp.float32).astype(jnp.bfloat16)
    slot = lax.broadcasted_iota(jnp.int32, (nz * fields, obs_count), 0)
    wanted = olevel[...] * fields + ofield[...]
    weight = oweight[...]
    mix[...] = jnp.where(slot == wanted, weight, jnp.where(slot == wanted + fields, 1.0 - weight, 0.0))

    def put_plane(target, s, plane, start=0):
        target[pl.ds(GROUP * start + s, plane.shape[0], stride=GROUP), :] = plane

    lat_count = ny * cy
    row_y = lax.broadcasted_iota(jnp.int32, (cy, LANES), 0) + gy * cy
    n_own = jnp.where(row_y == lat_count - 1, 0.0, diff[1, 0])
    for f in range(fields):
        put_plane(field_a, f, ctrl[f, 0], HALO)
        put_plane(rate_e, f, diff[0, 0], HALO)
        put_plane(rate_n, f, n_own, HALO)

    for copy in halo_copies:
        copy.wait()

    lane_x = lax.broadcasted_iota(jnp.int32, (rows, LANES), 1)

    def aux_plane(j):
        from_east = e_ext[...] if j == 0 else pltpu.roll(e_ext[...], LANES - HALO * j, 1)
        from_west = pltpu.roll(w_ext[...], LANES - HALO * (j + 1), 1)
        rest = jnp.where(lane_x >= LANES - HALO, from_west, 0.0)
        return jnp.where(lane_x < HALO, from_east, rest)

    row_x = lax.broadcasted_iota(jnp.int32, (rows, LANES), 0) + (gy * cy - HALO)
    wall = (row_x == lat_count - 1) | (row_x == -1)
    row_s = lax.broadcasted_iota(jnp.int32, (HALO, LANES), 0) + (gy * cy - HALO)
    e_aux = aux_plane(fields)
    n_aux = jnp.where(wall, 0.0, aux_plane(fields + 1))
    n_south = jnp.where(row_s == -1, 0.0, south_d[1])
    for f in range(fields):
        put_plane(field_a, f, south_c[f])
        put_plane(field_a, f, north_c[f], HALO + cy)
        put_plane(field_a, fields + f, aux_plane(f))
        put_plane(rate_e, f, south_d[0])
        put_plane(rate_e, f, north_d[0], HALO + cy)
        put_plane(rate_e, fields + f, e_aux)
        put_plane(rate_n, f, n_south)
        put_plane(rate_n, f, north_d[1], HALO + cy)
        put_plane(rate_n, fields + f, n_aux)

    margin = HALO - STEPS + 1
    span = rows - 2 * margin
    count = -(-span // BLOCK)
    edges = [margin + span * k // count for k in range(count + 1)]

    def swap(v):
        return pltpu.roll(v.reshape(-1, GROUP, LANES), fields, 1).reshape(v.shape)

    def lanes_of(v):
        return lax.broadcasted_iota(jnp.int32, v.shape, 1)

    def west_of(v, swapped):
        return pltpu.roll(jnp.where(lanes_of(v) == LANES - 1, swapped, v), 1, 1)

    for low_row, high_row in zip(edges[:-1], edges[1:]):
        size = (high_row - low_row) * GROUP
        here = pl.ds(low_row * GROUP, size)
        e = rate_e[here, :]
        n = rate_n[pl.ds((low_row - 1) * GROUP, size + GROUP), :]
        w = west_of(e, swap(e))
        rate_w[here, :] = w
        rate_0[here, :] = 1.0 - (e + w + n[GROUP:] + n[:-GROUP])

    def step(old, new):
        for low_row, high_row in zip(edges[:-1], edges[1:]):
            size = (high_row - low_row) * GROUP
            here = pl.ds(low_row * GROUP, size)
            n = rate_n[pl.ds((low_row - 1) * GROUP, size + GROUP), :]
            tall = old[pl.ds((low_row - 1) * GROUP, size + 2 * GROUP), :]
            v = tall[GROUP:-GROUP]
            swapped = swap(v)
            v_east = pltpu.roll(jnp.where(lanes_of(v) == 0, swapped, v), LANES - 1, 1)
            new[here, :] = (
                rate_0[here, :] * v
                + rate_e[here, :] * v_east
                + rate_w[here, :] * west_of(v, swapped)
                + n[GROUP:] * tall[2 * GROUP :]
                + n[:-GROUP] * tall[: -2 * GROUP]
            )

    def diffuse():
        @pl.loop(0, STEPS // 2)
        def _(_):
            step(field_a, field_b)
            step(field_b, field_a)

    diffuse()

    for f in range(fields):
        turned = field_a[pl.ds(GROUP * HALO + f, cy, stride=GROUP), :].T
        big, small = two_parts(turned)
        gather_lhs[pl.ds(f * cx, cx), 0:cy] = big.astype(jnp.bfloat16)
        gather_lhs[pl.ds(f * cx, cx), cy : 2 * cy] = small.astype(jnp.bfloat16)

    row_p = lax.broadcasted_iota(jnp.int32, (cy, profs), 0)

    def gather_for(tile):
        holder, cell = codes[tile, 0:1], codes[tile, 1:2]
        y, x = halves(cell, cx)
        y = jnp.where(holder == me, y, -1)
        pick = (row_p == y).astype(jnp.float32).astype(jnp.bfloat16)
        found = jnp.dot(
            gather_lhs[...],
            jnp.concatenate([pick, pick], axis=0),
            preferred_element_type=jnp.float32,
        )
        column = row_p == x
        sums = [
            jnp.sum(jnp.where(column, found[f * cx : (f + 1) * cx], 0.0), axis=0, keepdims=True)
            for f in range(fields)
        ]
        return jnp.concatenate(sums, axis=0)

    @pl.loop(1, tiles)
    def _(i):
        tile = other_tile(i)
        tile_copy(codes.at[tile], codes, code_send, code_recv, i, tile).wait_recv()

    together = 4 if tiles % 4 == 0 else 1

    @pl.loop(0, tiles // together)
    def _(g):
        for k in range(together):
            i = lax.rem(g * together + k + 1, tiles)
            gathered[i] = gather_for(other_tile(i))
        for k in range(together):
            i = g * together + k + 1

            @pl.when(i < tiles)
            def _():
                tile_copy(gathered.at[i], col_in, col_send, col_recv, i, me).start()

    @pl.loop(1, tiles)
    def _(i):
        tile = other_tile(i)
        tile_copy(gathered.at[i], col_in, col_send, col_recv, i, tile).wait_recv()
        gathered[0] = gathered[0] + col_in[tile]

    col_all[gz] = gathered[0]

    @pl.loop(1, nz)
    def _(i):
        level_copy(col_all.at[gz], col_all, lev_send, lev_recv, i, gz).start()

    row_r = lax.broadcasted_iota(jnp.int32, (rows, profs), 0)
    row_c = lax.broadcasted_iota(jnp.int32, (2 * LANES, profs), 0)

    @pl.loop(0, tiles)
    def _(tile):
        holder, cell = codes[tile, 0:1], codes[tile, 1:2]
        holder_x, _ = halves(holder, ny)
        _, x = halves(cell, cx)
        side = ((holder_x == east) & (x < cx // 2)) | ((holder_x == west) & (x >= cx // 2))
        place = jnp.where(holder_x == gx, x, jnp.where(side, LANES + x, -1))
        spots[tile] = (row_c == place).astype(jnp.float32).astype(jnp.bfloat16)

    @pl.loop(1, nz)
    def _(i):
        level = other_level(i)
        level_copy(col_all.at[level], col_all, lev_send, lev_recv, i, level).wait_recv()

    wide = nz * fields
    big, small = two_parts(col_all[...].reshape(wide, profs))
    both = jnp.concatenate([big, small], axis=0).astype(jnp.bfloat16)
    seen = jnp.dot(both, match[...], preferred_element_type=jnp.float32)
    seen = seen[0:wide] + seen[wide:]
    observed = jnp.sum(mix[...] * seen, axis=0, keepdims=True)
    departures = oprec[...] * (observed - innov[...])
    dep_out[...] = departures
    big, small = two_parts(mix[...] * departures)
    both = jnp.concatenate([big, small], axis=0).astype(jnp.bfloat16)
    back = lax.dot_general(
        both, match[...], (((1,), (1,)), ((), ())), preferred_element_type=jnp.float32
    )
    adj_part[...] = (back[0:wide] + back[wide:]).reshape(nz, fields, profs)

    @pl.loop(1, nz)
    def _(i):
        level_copy(adj_part.at[other_level(i)], adj_in, red_send, red_recv, i, gz).start()

    @pl.loop(0, tiles)
    def _(tile):
        holder, cell = codes[tile, 0:1], codes[tile, 1:2]
        _, holder_y = halves(holder, ny)
        y, _ = halves(cell, cx)
        near = row_r == (holder_y - gy) * cy + y + HALO
        nears[tile] = near.astype(jnp.float32).astype(jnp.bfloat16)

    gathered[0] = adj_part[gz]

    @pl.loop(1, nz)
    def _(i):
        level = other_level(i)
        level_copy(adj_part.at[level], adj_in, red_send, red_recv, i, level).wait_recv()
        gathered[0] = gathered[0] + adj_in[level]

    adj_all[me] = gathered[0]

    @pl.loop(1, tiles)
    def _(i):
        tile_copy(adj_all.at[me], adj_all, adj_send, adj_recv, i, me).start()

    def scatter_from(some):
        lines = [[] for _ in range(fields)]
        places = []
        for tile in some:
            near = nears[tile]
            for part in two_parts(adj_all[tile]):
                part = part.astype(jnp.bfloat16)
                places.append(spots[tile])
                for f in range(fields):
                    lines[f].append(near * part[f : f + 1])
        return lax.dot_general(
            jnp.concatenate([jnp.concatenate(line, axis=1) for line in lines], axis=0),
            jnp.concatenate(places, axis=1),
            (((1,), (1,)), ((), ())),
            preferred_element_type=jnp.float32,
        )

    spread[...] = scatter_from([me])
    joined = 7 if (tiles - 1) % 7 == 0 else 1

    @pl.loop(0, (tiles - 1) // joined)
    def _(g):
        some = [other_tile(g * joined + k + 1) for k in range(joined)]
        for k, tile in enumerate(some):
            i = g * joined + k + 1
            tile_copy(adj_all.at[me], adj_all, adj_send, adj_recv, i, tile).wait_recv()
        spread[...] += scatter_from(some)

    for f in range(fields):
        put_plane(field_a, f, spread[pl.ds(f * rows, rows), 0:LANES])
        put_plane(field_a, fields + f, spread[pl.ds(f * rows, rows), LANES : 2 * LANES])

    diffuse()

    for f in range(fields):
        grad_out[f, 0] = field_a[pl.ds(GROUP * HALO + f, cy, stride=GROUP), :]

    @pl.loop(1, tiles)
    def _(i):
        tile_copy(codes.at[me], codes, code_send, code_recv, i, me).wait_send()
        tile_copy(gathered.at[i], col_in, col_send, col_recv, i, me).wait_send()
        tile_copy(adj_all.at[me], adj_all, adj_send, adj_recv, i, me).wait_send()

    @pl.loop(1, nz)
    def _(i):
        level_copy(col_all.at[gz], col_all, lev_send, lev_recv, i, gz).wait_send()
        level_copy(adj_part.at[other_level(i)], adj_in, red_send, red_recv, i, gz).wait_send()


def per_device(
    nx, ny, nz,
    control,
    diffusivity,
    prof_tile,
    prof_cell,
    obs_prof,
    obs_field,
    obs_level,
    obs_weight,
    innovation,
    obs_precision,
):
    fields, _, cy, cx = control.shape
    profs = prof_cell.shape[0]
    obs_count = obs_prof.shape[0]
    tiles = nx * ny
    rows = cy + 2 * HALO
    f32 = jnp.float32

    def plane(*shape):
        return pltpu.VMEM(shape, f32)

    def flags(count):
        return pltpu.SemaphoreType.DMA((count,))

    def numbers(count):
        return pltpu.VMEM((1, count), jnp.int32)

    scratch = [
        plane(*control.shape), plane(*diffusivity.shape), numbers(profs), numbers(profs),
        numbers(obs_count), numbers(obs_count), numbers(obs_count),
        plane(1, obs_count), plane(1, obs_count), plane(1, obs_count), flags(10),
        pltpu.VMEM((profs, obs_count), jnp.bfloat16), plane(nz * fields, obs_count),
    ]
    scratch += [
        plane(cy, LANES), plane(cy, LANES), plane(rows, LANES), plane(rows, LANES),
        plane(fields, HALO, LANES), plane(fields, HALO, LANES),
        plane(2, HALO, LANES), plane(2, HALO, LANES),
        pltpu.VMEM((tiles, 2, profs), jnp.int32),
    ]
    scratch += [plane(rows * GROUP, LANES)] * 6
    scratch += [
        pltpu.VMEM((fields * cx, 2 * cy), jnp.bfloat16),
        plane(tiles, fields, profs),
        plane(tiles, fields, profs),
        plane(nz, fields, profs),
        plane(nz, fields, profs),
        plane(nz, fields, profs),
        plane(tiles, fields, profs),
        plane(fields * rows, 2 * LANES),
        pltpu.VMEM((tiles, 2 * LANES, profs), jnp.bfloat16),
        pltpu.VMEM((tiles, rows, profs), jnp.bfloat16),
        flags(10), flags(10),
        flags(tiles), flags(tiles), flags(tiles), flags(tiles),
        flags(nz), flags(nz), flags(nz), flags(nz),
        flags(tiles), flags(tiles),
    ]
    spread, departures = pl.pallas_call(
        functools.partial(kernel, nx, ny, nz),
        out_shape=(
            jax.ShapeDtypeStruct(control.shape, f32),
            jax.ShapeDtypeStruct((1, obs_count), f32),
        ),
        in_specs=[pl.BlockSpec(memory_space=pltpu.HBM)] * 10,
        out_specs=(pl.BlockSpec(memory_space=pltpu.VMEM),) * 2,
        scratch_shapes=scratch,
        compiler_params=pltpu.CompilerParams(
            collective_id=0, has_side_effects=True, vmem_limit_bytes=(64 * 1024 - 750) * 1024
        ),
    )(
        control,
        diffusivity,
        prof_tile.reshape(1, profs),
        prof_cell.reshape(1, profs),
        obs_prof.reshape(1, obs_count),
        obs_field.reshape(1, obs_count),
        obs_level.reshape(1, obs_count),
        obs_weight.reshape(1, obs_count),
        innovation.reshape(1, obs_count),
        obs_precision.reshape(1, obs_count),
    )
    return (control + spread, departures.reshape(obs_count))


def solution(mesh):
    nx, ny, nz = mesh.shape["gx"], mesh.shape["gy"], mesh.shape["obs"]
    in_specs = (
        P(None, "obs", "gy", "gx"),
        P(None, "obs", "gy", "gx"),
        P(("gx", "gy"), None),
        P(("gx", "gy")),
        P(("gx", "gy", "obs")),
        P(("gx", "gy", "obs")),
        P(("gx", "gy", "obs")),
        P(("gx", "gy", "obs")),
        P(("gx", "gy", "obs")),
        P(("gx", "gy", "obs")),
    )
    out_specs = (P(None, "obs", "gy", "gx"), P(("gx", "gy", "obs")))
    return jax.shard_map(
        functools.partial(per_device, nx, ny, nz),
        mesh=mesh,
        in_specs=in_specs,
        out_specs=out_specs,
        check_vma=False,
    )
```
